512 devices in a mesh: grp: 4 (over x), seq: 16 (over y, core), tp: 8 (over z).
Axes of the slice: x: 4, y: 8, z: 8, core: 2. Of those that a mesh axis runs over, the one named last changes fastest.
Arguments:
- byte_states: bfloat16 [4, 4096, 1024], P('grp', 'seq', 'tp'), may hold values from -6 to 6
- patch_map: int32 [4, 4096], P('grp', 'seq'), may hold values from 0 to 63, as said below
- lift_weight: bfloat16 [1024, 4096], P('tp'), may hold values from -0.1875 to 0.1875
- gate_weight: bfloat16 [4096, 8192], P('seq', ('grp', 'tp')), may hold values from -0.09375 to 0.09375
- up_weight: bfloat16 [4096, 8192], P('seq', ('grp', 'tp')), may hold values from -0.09375 to 0.09375
- down_weight: bfloat16 [8192, 4096], P(('grp', 'tp'), 'seq'), may hold values from -0.0625 to 0.0625
- return_weight: bfloat16 [4096, 1024], P(None, 'tp'), may hold values from -0.09375 to 0.09375
Outputs:
- byte_output: bfloat16 [4, 4096, 1024], P('grp', 'seq', 'tp')
The draws below stay inside these ranges and needn't reach their ends.
Inputs may be any that keep to these rules, and one draw needn't show every extreme that they name: `patch_map`: within each block of 256 bytes the values never fall, start at 0 and take every value from 0 to n - 1, with n one of 64, 32, 16, 8; in every sequence some block has n = 64.
All inputs are finite; a program needn't handle non-finite values.
Results may differ from the reference program's by a relative error of at most 0.025.
Values may be sent and summed in bfloat16 or wider, within the bound.
A program may use at most 64 MiB of HBM per device.

```python
import jax
import jax.numpy as jnp
from jax import lax

DL = 1024
DG = 4096
FF = 8192
BYTES_DEV = 256
NMAX = 64
SEQS = 4
BYTES = 4096
FF_BLOCK = 256
N_SEQ = 16


def draw_patch_map(key, part):
    key = jax.random.fold_in(key, 7)
    halving_key, full_key, score_key = jax.random.split(key, 3)
    halvings = jax.random.randint(halving_key, (SEQS, N_SEQ), 0, 4)
    full_block = jax.random.randint(full_key, (SEQS, 1), 0, N_SEQ)
    halvings = jnp.where(jnp.arange(N_SEQ)[None, :] == full_block, 0, halvings)
    live_count = NMAX // jnp.left_shift(jnp.ones_like(halvings), halvings)
    random_score = jax.random.randint(score_key, (SEQS, N_SEQ, BYTES_DEV - 1), 0, 65536) * 4096
    random_score = random_score + jnp.arange(BYTES_DEV - 1, dtype=jnp.int32)
    order_rank = jnp.argsort(jnp.argsort(random_score, axis=-1, stable=True), axis=-1, stable=True)
    cut_flags = (order_rank < (live_count - 1)[..., None]).astype(jnp.int32)
    slot_ids = jnp.concatenate([jnp.zeros((SEQS, N_SEQ, 1), jnp.int32), jnp.cumsum(cut_flags, axis=-1).astype(jnp.int32)], axis=-1)
    return slot_ids.reshape(SEQS, N_SEQ * BYTES_DEV).astype(jnp.int32)


def levels(rng, dims, pieces, least, largest):
    def one(dim, shards_of):
        heights = jax.random.uniform(jax.random.fold_in(jax.random.fold_in(rng, 6), dim), (shards_of,), jnp.float32, least / len(pieces), largest / len(pieces))
        return jnp.repeat(jnp.exp(heights), dims[dim] // shards_of).reshape((-1,) + (1,) * (len(dims) - dim - 1))

    level = one(*pieces[0])
    for cut in pieces[1:]:
        level = level * one(*cut)
    return level


def bell_draw(rng, dims, deviation, reach, cuts=(), held_as=jnp.bfloat16):
    entries = jax.random.normal(rng, dims, jnp.float32) * deviation
    if len(cuts) > 0:
        entries = levels(rng, dims, cuts, -0.22, 0.18) * entries
    return jnp.clip(entries, min=-reach, max=reach).astype(held_as)


def setup_inputs(seed: int = 0) -> dict:
    key_of = jax.random.split(jax.random.key(seed), 8)
    byte_states = bell_draw(key_of[0], (SEQS, BYTES, DL), 1.0, 6.0, ((0, 4), (1, 16), (2, 8)))
    patch_map = draw_patch_map(jax.random.fold_in(key_of[7], 71), 0)
    lift_weight = bell_draw(key_of[2], (DL, DG), DL ** -0.5, 0.1875, ((0, 8),))
    gate_weight = bell_draw(key_of[3], (DG, FF), DG ** -0.5, 0.09375, ((0, 16), (1, 32)))
    up_weight = bell_draw(key_of[4], (DG, FF), DG ** -0.5, 0.09375, ((0, 16), (1, 32)))
    down_weight = bell_draw(key_of[5], (FF, DG), FF ** -0.5, 0.0625, ((0, 32), (1, 16)))
    return_weight = bell_draw(key_of[6], (DG, DL), DG ** -0.5, 0.09375, ((1, 8),))
    return dict(byte_states=byte_states, patch_map=patch_map, lift_weight=lift_weight, gate_weight=gate_weight, up_weight=up_weight, down_weight=down_weight, return_weight=return_weight)


epsilon = 1e-05

def reference(byte_states, patch_map, lift_weight, gate_weight, up_weight, down_weight, return_weight):
    states = byte_states.reshape(SEQS, N_SEQ, BYTES_DEV, DL)
    slot_ids = patch_map.reshape(SEQS, N_SEQ, BYTES_DEV)
    onehot = (slot_ids[..., None] == jnp.arange(NMAX, dtype=jnp.int32)).astype(jnp.float32)
    counts = lax.optimization_barrier(jnp.sum(onehot, axis=2))
    byte_sums = jnp.einsum('gnbp,gnbd->gnpd', onehot, states.astype(jnp.float32))
    pooled = (byte_sums / jnp.maximum(counts, 1.0)[..., None]).astype(jnp.bfloat16)
    pooled = pooled.reshape(SEQS * N_SEQ * NMAX, DL)
    patch_in = jnp.dot(pooled, lift_weight, preferred_element_type=jnp.float32).astype(jnp.bfloat16)
    widened = patch_in.astype(jnp.float32)
    normed = (widened * lax.rsqrt(lax.optimization_barrier(jnp.mean(widened * widened, axis=1, keepdims=True)) + epsilon)).astype(jnp.bfloat16)
    gate_act = jnp.dot(normed, gate_weight, preferred_element_type=jnp.float32)
    up_act = jnp.dot(normed, up_weight, preferred_element_type=jnp.float32)
    hidden = (jax.nn.silu(gate_act) * up_act).astype(jnp.bfloat16)

    def add_block(block_index, running):
        first = block_index * FF_BLOCK
        hidden_block = lax.dynamic_slice_in_dim(hidden, first, FF_BLOCK, 1)
        down_block = lax.dynamic_slice_in_dim(down_weight, first, FF_BLOCK, 0)
        rounded = jnp.dot(hidden_block, down_block, preferred_element_type=jnp.float32).astype(jnp.bfloat16)
        rounded = lax.optimization_barrier(rounded)
        return running + rounded.astype(jnp.float32)
    latent_delta = lax.fori_loop(0, FF // FF_BLOCK, add_block, jnp.zeros((SEQS * N_SEQ * NMAX, DG), jnp.float32))
    patch_out = (widened + latent_delta).astype(jnp.bfloat16)
    returned = jnp.dot(patch_out, return_weight, preferred_element_type=jnp.float32).astype(jnp.bfloat16)
    returned = returned.reshape(SEQS, N_SEQ, NMAX, DL)
    spread = jnp.einsum('gnbp,gnpd->gnbd', onehot, returned.astype(jnp.float32))
    mixed_rows = states.astype(jnp.float32) + spread
    scaled = mixed_rows * lax.rsqrt(lax.optimization_barrier(jnp.mean(mixed_rows * mixed_rows, axis=-1, keepdims=True)) + epsilon)
    return scaled.astype(jnp.bfloat16).reshape(SEQS, BYTES, DL)
```

```python
import jax
import jax.numpy as jnp
from jax import lax
from jax.experimental import pallas as pl
from jax.experimental.pallas import tpu as pltpu
from jax.sharding import PartitionSpec as P

DL = 1024
NMAX = 64
EPS = 1e-05
MESH = pl.DeviceIdType.MESH
F32 = jnp.float32
BF16 = jnp.bfloat16
OUT_ORDER = (4, 3, 5, 2, 6, 1, 7, 0)
IN_ORDER = (0, 1, 7, 2, 6, 3, 5, 4)


def dot(a, b):
    return jnp.dot(a, b, preferred_element_type=F32)


def kernel(
    states_ref, map_ref, lift_hbm, gate_hbm, up_hbm, down_hbm, ret_hbm, out_ref,
    lift, weights, lift_out, lift_in, patch, acc, part, half_in, pair_out, pair_in,
    done_out, done_in, ret, back_out, back_in, sq_out, sq_in,
    load_sem, y_send, y_recv, sib_send, sib_recv, lift_send, lift_recv,
    zg_send, zg_recv, xg_send, xg_recv, ret_send, ret_recv, rsib_send, rsib_recv,
    h_send, h_recv, p_send, p_recv, d_send, d_recv, b_send, b_recv, q_send, q_recv,
):
    x = lax.axis_index("grp")
    s = lax.axis_index("seq")
    z = lax.axis_index("tp")
    y = s // 2
    c = s % 2
    xa = x + 1 - 2 * (x % 2)
    xb = 3 - x
    sib = 2 * y + 1 - c
    started = []

    def z_at(d):
        return (z + d + 8) % 8

    def slot(q):
        return 2 * ((y + q + 8) % 8) + c

    def remote(src, dst, ss, rs, device):
        return pltpu.make_async_remote_copy(
            src_ref=src, dst_ref=dst, send_sem=ss, recv_sem=rs,
            device_id=device, device_id_type=MESH,
        )

    def send(src, dst, ss, rs, device):
        copy = remote(src, dst, ss, rs, device)
        copy.start()
        started.append(copy)

    def arrived(ref, ss, rs, device):
        remote(ref, ref, ss, rs, device).wait_recv()

    loads = [
        pltpu.make_async_copy(gate_hbm, weights.at[s, 0], load_sem.at[0]),
        pltpu.make_async_copy(up_hbm, weights.at[s, 1], load_sem.at[1]),
        pltpu.make_async_copy(down_hbm, weights.at[s, 2], load_sem.at[2]),
        pltpu.make_async_copy(lift_hbm, lift, load_sem.at[3]),
        pltpu.make_async_copy(ret_hbm.at[pl.ds(z * 512, 512)], ret.at[0], load_sem.at[4]),
    ]
    for load in loads:
        load.start()
    barrier = pltpu.get_barrier_semaphore()
    partners = [{"seq": slot(1)}, {"seq": slot(-1)}, {"seq": sib}, {"grp": xa}, {"grp": xb}]
    partners += [{"tp": z_at(d)} for d in range(1, 8)]
    for partner in partners:
        pl.semaphore_signal(barrier, inc=1, device_id=partner, device_id_type=MESH)
    pl.semaphore_wait(barrier, len(partners))
    for load in loads[:3]:
        load.wait()

    def y_ref(q, st, way, hop):
        rows = pl.ds(0, 256) if hop < 3 else pl.ds(128 * way, 128)
        first, count = ((0, 2), (2, 1))[st]
        return weights.at[slot(q), pl.ds(first, count), rows]

    def y_go(way, hop, st):
        q = -hop if way == 0 else hop
        ref = y_ref(q, st, way, hop)
        send(ref, ref, y_send.at[way, hop, st], y_recv.at[way, hop, st],
             {"seq": slot(1 if way == 0 else -1)})

    def sib_go(q, st):
        ref = y_ref(q, st, 0, 0)
        k = q % 8
        send(ref, ref, sib_send.at[k, st], sib_recv.at[k, st], {"seq": sib})

    def y_start():
        for st in (0, 1):
            y_go(0, 0, st)
            y_go(1, 0, st)
            sib_go(0, st)

    def y_step(hop, st):
        for way in (0, 1):
            q = -(hop + 1) if way == 0 else hop + 1
            arrived(y_ref(q, st, way, hop), y_send.at[way, hop, st], y_recv.at[way, hop, st],
                    {"seq": slot(1)})
            if hop < 3:
                y_go(way, hop + 1, st)
                sib_go(q, st)
        if hop == 3:
            sib_go(4, st)

    def sib_wait(st):
        first, count = ((0, 2), (2, 1))[st]
        for k in range(8):
            ref = weights.at[2 * ((y + k) % 8) + 1 - c, pl.ds(first, count)]
            arrived(ref, sib_send.at[k, st], sib_recv.at[k, st], {"seq": sib})

    y_start()

    map_row = map_ref[...]
    onehot = (lax.broadcasted_iota(jnp.int32, (NMAX, 256), 0) == map_row).astype(F32)
    counts = jnp.sum(onehot, axis=1, keepdims=True)
    states = states_ref[...]
    sums = dot(onehot.astype(BF16), states)
    pooled = (sums / jnp.maximum(counts, 1.0)).astype(BF16)
    loads[3].wait()
    for k in range(8):
        lift_out[k] = dot(pooled, lift[:, 512 * k : 512 * (k + 1)]).astype(BF16)
    for d in (4, 3, 5, 2, 6, 1, 7):
        send(lift_out.at[z_at(d)], lift_in.at[d], lift_send.at[d], lift_recv.at[d],
             {"tp": z_at(d)})

    y_step(0, 0)
    y_step(0, 1)

    block = lift_out[z].astype(F32)
    for d in (1, 7, 2, 6, 3, 5, 4):
        arrived(lift_in.at[d], lift_send.at[d], lift_recv.at[d], {"tp": z_at(d)})
        block = block + lift_in[d].astype(F32)
    patch[0, 0] = block.astype(BF16)

    def zg_ref(e, way, hop):
        rows = pl.ds(0, 64) if hop < 3 else pl.ds(32 * way, 32)
        return patch.at[e, 0, rows]

    def zg_go(way, hop):
        e = hop if way == 0 else (8 - hop) % 8
        e2 = hop + 1 if way == 0 else 7 - hop
        send(zg_ref(e, way, hop), zg_ref(e2, way, hop), zg_send.at[way, hop],
             zg_recv.at[way, hop], {"tp": z_at(1 if way == 0 else -1)})

    def zg_wait(way, hop):
        e = hop + 1 if way == 0 else 7 - hop
        arrived(zg_ref(e, way, hop), zg_send.at[way, hop], zg_recv.at[way, hop],
                {"tp": z_at(1)})

    def first_second(i):
        return ((xa, 1), (xb, 3)) if i % 2 == 0 else ((xb, 3), (xa, 1))

    def xg_one(i):
        e = IN_ORDER[i]
        (n1, j1), _ = first_second(i)
        send(patch.at[e, 0], patch.at[e, j1], xg_send.at[e, 0], xg_recv.at[e, 0], {"grp": n1})

    def xg_two(i):
        e = IN_ORDER[i]
        (n1, j1), (n2, j2) = first_second(i)
        send(patch.at[e, 0], patch.at[e, j2], xg_send.at[e, 1], xg_recv.at[e, 1], {"grp": n2})
        arrived(patch.at[e, j1], xg_send.at[e, 0], xg_recv.at[e, 0], {"grp": n1})
        send(patch.at[e, j1], patch.at[e, 2], xg_send.at[e, 2], xg_recv.at[e, 2], {"grp": n2})

    def xg_wait(i):
        e = IN_ORDER[i]
        _, (n2, j2) = first_second(i)
        arrived(patch.at[e, j2], xg_send.at[e, 1], xg_recv.at[e, 1], {"grp": n2})
        arrived(patch.at[e, 2], xg_send.at[e, 2], xg_recv.at[e, 2], {"grp": n2})

    zg_go(0, 0)
    zg_go(1, 0)
    xg_one(0)
    y_step(1, 0)
    zg_wait(0, 0)
    zg_go(0, 1)
    xg_one(1)
    zg_wait(1, 0)
    zg_go(1, 1)
    xg_one(2)
    xg_two(0)
    y_step(1, 1)
    zg_wait(0, 1)
    zg_go(0, 2)
    xg_one(3)
    zg_wait(1, 1)
    zg_go(1, 2)
    xg_one(4)
    xg_two(1)
    xg_two(2)
    y_step(2, 0)
    zg_wait(0, 2)
    zg_go(0, 3)
    xg_one(5)
    zg_wait(1, 2)
    zg_go(1, 3)
    xg_one(6)
    xg_two(3)
    xg_two(4)
    y_step(2, 1)
    zg_wait(0, 3)
    zg_wait(1, 3)
    xg_one(7)

    half = pl.ds(256 * c, 256)
    other = pl.ds(256 * (1 - c), 256)
    for d in (4, 3, 5, 2, 6, 1, 7):
        send(ret_hbm.at[pl.ds(z_at(d) * 512 + 256 * c, 256)], ret.at[d, half],
             ret_send.at[d], ret_recv.at[d], {"tp": z_at(d)})

    xg_two(5)
    xg_two(6)
    y_step(3, 0)
    y_step(3, 1)
    xg_two(7)
    sib_wait(0)

    squares = jnp.zeros((256, 1), F32)
    for i in range(8):
        e = IN_ORDER[i]
        if i > 0:
            xg_wait(i)
        else:
            xg_wait(0)
        kb = z_at(-e)
        rows = patch[e].reshape(256, 512)
        wide = rows.astype(F32)
        squares = squares + jnp.sum(wide * wide, axis=1, keepdims=True)
        for a in (0, 1):
            w = weights[pl.ds(2 * kb, 2), a].reshape(512, 256)
            if i == 0:
                acc[a] = dot(rows, w)
            else:
                acc[a] += dot(rows, w)
    scale = lax.rsqrt(squares * (1.0 / 4096) + EPS)
    gate = acc[0] * scale
    up = acc[1] * scale
    hidden = (gate / (1.0 + jnp.exp(-gate)) * up).astype(BF16)

    sib_wait(1)

    def down_one(i):
        kb = z_at(OUT_ORDER[i])
        for n in (0, 1):
            val = dot(hidden, weights[2 * kb + n, 2]).astype(BF16)
            part[i, :, :, 256 * n : 256 * (n + 1)] = val.reshape(4, 64, 256)
        (n1, j1), _ = first_second(i)
        src = part.at[i, pl.ds(1 if j1 == 1 else 2, 2)]
        send(src, half_in.at[i], h_send.at[i], h_recv.at[i], {"grp": n1})

    def down_two(i):
        (n1, j1), (n2, j2) = first_second(i)
        arrived(half_in.at[i], h_send.at[i], h_recv.at[i], {"grp": n1})
        other_row = 1 if j1 == 1 else 0
        pair_out[i] = (part[i, j2].astype(F32) + half_in[i, other_row].astype(F32)).astype(BF16)
        send(pair_out.at[i], pair_in.at[i], p_send.at[i], p_recv.at[i], {"grp": n2})

    def down_three(i):
        (n1, j1), (n2, j2) = first_second(i)
        arrived(pair_in.at[i], p_send.at[i], p_recv.at[i], {"grp": n2})
        own_row = 0 if j1 == 1 else 1
        total = (
            part[i, 0].astype(F32) + half_in[i, own_row].astype(F32) + pair_in[i].astype(F32)
        )
        d = OUT_ORDER[i]
        if d == 0:
            return total
        done_out[i] = total.astype(BF16)
        send(done_out.at[i], done_in.at[d], d_send.at[d], d_recv.at[d], {"tp": z_at(d)})
        return None

    for i in range(8):
        down_one(i)
    delta = None
    for i in range(9):
        if i < 8:
            down_two(i)
        if i > 0:
            delta = down_three(i - 1)

    loads[4].wait()
    for d in range(1, 8):
        arrived(ret.at[d, half], ret_send.at[d], ret_recv.at[d], {"tp": z_at(d)})
    send(ret.at[pl.ds(1, 7), half], ret.at[pl.ds(1, 7), half], rsib_send, rsib_recv, {"seq": sib})

    for d in (1, 7, 2, 6, 3, 5, 4):
        arrived(done_in.at[d], d_send.at[d], d_recv.at[d], {"tp": z_at(d)})
        delta = delta + done_in[d].astype(F32)
    patch_out = (patch[0, 0].astype(F32) + delta).astype(BF16)
    arrived(ret.at[pl.ds(1, 7), other], rsib_send, rsib_recv, {"seq": sib})
    for d in (4, 3, 5, 2, 6, 1, 7):
        back_out[d] = dot(patch_out, ret[d]).astype(BF16)
        send(back_out.at[d], back_in.at[d], b_send.at[d], b_recv.at[d], {"tp": z_at(-d)})
    returned = dot(patch_out, ret[0])
    for d in (1, 7, 2, 6, 3, 5, 4):
        arrived(back_in.at[d], b_send.at[d], b_recv.at[d], {"tp": z_at(d)})
        returned = returned + back_in[d].astype(F32)
    returned = returned.astype(BF16)

    spread = lax.dot_general(
        onehot.astype(BF16), returned, (((0,), (0,)), ((), ())), preferred_element_type=F32
    )
    mixed = states.astype(F32) + spread
    ones = jnp.ones((8, 128), F32)
    sq_out[...] = lax.dot_general(
        ones, mixed * mixed, (((1,), (1,)), ((), ())),
        precision=lax.Precision.HIGHEST, preferred_element_type=F32,
    )
    for d in (4, 3, 5, 2, 6, 1, 7):
        send(sq_out, sq_in.at[d], q_send.at[d], q_recv.at[d], {"tp": z_at(d)})
    total = sq_out[...]
    for d in (1, 7, 2, 6, 3, 5, 4):
        arrived(sq_in.at[d], q_send.at[d], q_recv.at[d], {"tp": z_at(d)})
        total = total + sq_in[d]
    spread_sum = lax.dot_general(
        total, ones * 0.125, (((0,), (0,)), ((), ())),
        precision=lax.Precision.HIGHEST, preferred_element_type=F32,
    )
    out_ref[...] = (mixed * lax.rsqrt(spread_sum * (1.0 / DL) + EPS)).astype(BF16)
    for copy in started:
        copy.wait_send()


def on_device(
    byte_states, patch_map, lift_weight, gate_weight, up_weight, down_weight, return_weight
):
    vmem = pl.BlockSpec(memory_space=pltpu.VMEM)
    hbm = pl.BlockSpec(memory_space=pl.ANY)
    dma = pltpu.SemaphoreType.DMA
    out = pl.pallas_call(
        kernel,
        out_shape=jax.ShapeDtypeStruct((256, 128), BF16),
        in_specs=[vmem, vmem, hbm, hbm, hbm, hbm, hbm],
        out_specs=vmem,
        scratch_shapes=[
            pltpu.VMEM((128, 4096), BF16),
            pltpu.VMEM((16, 3, 256, 256), BF16),
            pltpu.VMEM((8, 64, 512), BF16),
            pltpu.VMEM((8, 64, 512), BF16),
            pltpu.VMEM((8, 4, 64, 512), BF16),
            pltpu.VMEM((2, 256, 256), F32),
            pltpu.VMEM((8, 4, 64, 512), BF16),
            pltpu.VMEM((8, 2, 64, 512), BF16),
            pltpu.VMEM((8, 64, 512), BF16),
            pltpu.VMEM((8, 64, 512), BF16),
            pltpu.VMEM((8, 64, 512), BF16),
            pltpu.VMEM((8, 64, 512), BF16),
            pltpu.VMEM((8, 512, 128), BF16),
            pltpu.VMEM((8, 64, 128), BF16),
            pltpu.VMEM((8, 64, 128), BF16),
            pltpu.VMEM((8, 256), F32),
            pltpu.VMEM((8, 8, 256), F32),
            dma((5,)),
            dma((2, 4, 2)), dma((2, 4, 2)),
            dma((8, 2)), dma((8, 2)),
            dma((8,)), dma((8,)),
            dma((2, 4)), dma((2, 4)),
            dma((8, 3)), dma((8, 3)),
            dma((8,)), dma((8,)),
            dma, dma,
            dma((8,)), dma((8,)),
            dma((8,)), dma((8,)),
            dma((8,)), dma((8,)),
            dma((8,)), dma((8,)),
            dma((8,)), dma((8,)),
        ],
        compiler_params=pltpu.CompilerParams(
            collective_id=0, has_side_effects=True, vmem_limit_bytes=48 * 1024 * 1024
        ),
    )(byte_states[0], patch_map, lift_weight, gate_weight, up_weight, down_weight, return_weight)
    return out[None]


def solution(mesh):
    placed = (
        P("grp", "seq", "tp"),
        P("grp", "seq"),
        P("tp", None),
        P("seq", ("grp", "tp")),
        P("seq", ("grp", "tp")),
        P(("grp", "tp"), "seq"),
        P(None, "tp"),
    )
    return jax.shard_map(
        on_device, mesh=mesh, in_specs=placed, out_specs=P("grp", "seq", "tp"), check_vma=False
    )
```

```python
import jax
import jax.numpy as jnp
from jax import lax
from jax.experimental import pallas as pl
from jax.experimental.pallas import tpu as pltpu
from jax.sharding import PartitionSpec as P

DL = 1024
NMAX = 64
EPS = 1e-05
MESH = pl.DeviceIdType.MESH
F32 = jnp.float32
BF16 = jnp.bfloat16
IN_ORDER = (0, 1, 7, 2, 6, 3, 5, 4)


def dot(a, b):
    return jnp.dot(a, b, preferred_element_type=F32)


def kernel(
    states_ref, map_ref, lift_hbm, gate_hbm, up_hbm, down_hbm, ret_hbm, out_ref,
    lift, weights, lift_out, lift_in, patch, acc, down, ret, ret_rows, dr_own, dr_sib,
    dr_half, dr_in, dr, part, half_in, pair_out, pair_in, back_out, back_in, sq_out, sq_in,
    load_sem,
    y_sends, y_recvs,
    sib_sends, sib_recvs,
    lift_sends, lift_recvs,
    zg_sends, zg_recvs,
    xg_sends, xg_recvs,
    rz_sends, rz_recvs,
    rx_sends, rx_recvs,
    ds_sends, ds_recvs,
    dy_sends, dy_recvs,
    dg_sends, dg_recvs,
    dh_sends, dh_recvs,
    h_sends, h_recvs,
    p_sends, p_recvs,
    b_sends, b_recvs,
    q_sends, q_recvs,
):
    x = lax.axis_index("grp")
    s = lax.axis_index("seq")
    z = lax.axis_index("tp")
    y = s // 2
    c = s % 2
    xa = x + 1 - 2 * (x % 2)
    xb = 3 - x
    sib = 2 * y + 1 - c
    started = []
    y_sems = (y_sends, y_recvs)
    sib_sems = (sib_sends, sib_recvs)
    lift_sems = (lift_sends, lift_recvs)
    zg_sems = (zg_sends, zg_recvs)
    xg_sems = (xg_sends, xg_recvs)
    rz_sems = (rz_sends, rz_recvs)
    rx_sems = (rx_sends, rx_recvs)
    ds_sems = (ds_sends, ds_recvs)
    dy_sems = (dy_sends, dy_recvs)
    dg_sems = (dg_sends, dg_recvs)
    dh_sems = (dh_sends, dh_recvs)
    h_sems = (h_sends, h_recvs)
    p_sems = (p_sends, p_recvs)
    b_sems = (b_sends, b_recvs)
    q_sems = (q_sends, q_recvs)

    def z_at(d):
        return (z + d + 8) % 8

    def slot(q):
        return 2 * ((y + q + 8) % 8) + c

    def remote(src, dst, sems, index, device):
        return pltpu.make_async_remote_copy(
            src_ref=src, dst_ref=dst, send_sem=sems[0].at[index], recv_sem=sems[1].at[index],
            device_id=device, device_id_type=MESH,
        )

    def send(src, dst, sems, index, device):
        copy = remote(src, dst, sems, index, device)
        copy.start()
        started.append(copy)

    def arrived(ref, sems, index, device):
        remote(ref, ref, sems, index, device).wait_recv()

    loads = [
        pltpu.make_async_copy(lift_hbm, lift, load_sem.at[0]),
        pltpu.make_async_copy(gate_hbm, weights.at[s, 0], load_sem.at[1]),
        pltpu.make_async_copy(up_hbm, weights.at[s, 1], load_sem.at[2]),
        pltpu.make_async_copy(down_hbm, down, load_sem.at[3]),
        pltpu.make_async_copy(ret_hbm, ret, load_sem.at[4]),
    ]
    for load in loads:
        load.start()
    barrier = pltpu.get_barrier_semaphore()
    partners = [{"seq": slot(d)} for d in range(1, 8)] + [{"seq": sib}]
    partners += [{"grp": xa}, {"grp": xb}, {"grp": (x + 2) % 4}]
    partners += [{"tp": z_at(d)} for d in range(1, 8)]
    for partner in partners:
        pl.semaphore_signal(barrier, inc=1, device_id=partner, device_id_type=MESH)

    map_row = map_ref[...]
    onehot = (lax.broadcasted_iota(jnp.int32, (NMAX, 256), 0) == map_row).astype(F32)
    counts = jnp.sum(onehot, axis=1, keepdims=True)
    states = states_ref[...]
    sums = dot(onehot.astype(BF16), states)
    pooled = (sums / jnp.maximum(counts, 1.0)).astype(BF16)
    loads[0].wait()
    for k in range(8):
        lift_out[k] = dot(pooled, lift[:, 512 * k : 512 * (k + 1)]).astype(BF16)
    for load in loads[1:]:
        load.wait()
    pl.semaphore_wait(barrier, len(partners))

    def y_ref(q, way, hop):
        rows = pl.ds(0, 256) if hop < 3 else pl.ds(128 * way, 128)
        return weights.at[slot(q), :, rows]

    def y_go(way, hop):
        ref = y_ref(-hop if way == 0 else hop, way, hop)
        send(ref, ref, y_sems, (way, hop), {"seq": slot(1 if way == 0 else -1)})

    def sib_go(q):
        ref = weights.at[slot(q)]
        send(ref, ref, sib_sems, (q % 8,), {"seq": sib})

    def y_step(hop):
        for way in (0, 1):
            q = -(hop + 1) if way == 0 else hop + 1
            arrived(y_ref(q, way, hop), y_sems, (way, hop), {"seq": slot(1)})
            if hop < 3:
                y_go(way, hop + 1)
                sib_go(q)
        if hop == 3:
            sib_go(4)

    def sib_wait():
        for k in range(8):
            arrived(weights.at[2 * ((y + k) % 8) + 1 - c], sib_sems, (k,), {"seq": sib})

    quarter = pl.ds(64 * x, 64)
    own_rows = pl.ds(256 * s + 64 * x, 64)
    for d in (4, 3, 5, 2, 6, 1, 7):
        send(ret.at[own_rows], ret_rows.at[d, quarter], rz_sems, (d,), {"tp": z_at(d)})
    y_go(0, 0)
    y_go(1, 0)
    sib_go(0)
    for d in (4, 3, 5, 2, 6, 1, 7):
        send(lift_out.at[z_at(d)], lift_in.at[d], lift_sems, (d,), {"tp": z_at(d)})
    ret_rows[0, quarter] = ret[own_rows]
    for d in (1, 7, 2, 6, 3, 5, 4):
        arrived(ret_rows.at[d, quarter], rz_sems, (d,), {"tp": z_at(d)})
    for j in (2, 1, 3):
        ref = ret_rows.at[:, quarter]
        send(ref, ref, rx_sems, (j,), {"grp": (x + j) % 4})

    y_step(0)

    for j in (1, 3, 2):
        arrived(ret_rows.at[:, quarter], rx_sems, (j,), {"grp": xa})
    down_own = down[...]
    for d in range(8):
        dr_own[d] = dot(down_own, ret_rows[d]).astype(BF16)
    mine = pl.ds(4 * c, 4)
    send(dr_own.at[pl.ds(4 - 4 * c, 4)], dr_sib, ds_sems, (0,), {"seq": sib})
    arrived(dr_sib, ds_sems, (0,), {"seq": sib})
    dr_half[...] = (dr_own[mine].astype(F32) + dr_sib[...].astype(F32)).astype(BF16)

    def units(q):
        return pl.ds(32 * ((y + q + 8) % 8), 32)

    for q in (4, 3, 5, 2, 6, 1, 7):
        send(dr_half.at[:, units(q)], dr_in.at[q], dy_sems, (q,), {"seq": slot(q)})

    block = lift_out[z].astype(F32)
    for d in (1, 7, 2, 6, 3, 5, 4):
        arrived(lift_in.at[d], lift_sems, (d,), {"tp": z_at(d)})
        block = block + lift_in[d].astype(F32)
    patch[0, 0] = block.astype(BF16)

    def zg_ref(e, way, hop):
        rows = pl.ds(0, 64) if hop < 3 else pl.ds(32 * way, 32)
        return patch.at[e, 0, rows]

    def zg_go(way, hop):
        e = hop if way == 0 else (8 - hop) % 8
        e2 = hop + 1 if way == 0 else 7 - hop
        send(zg_ref(e, way, hop), zg_ref(e2, way, hop), zg_sems, (way, hop,), {"tp": z_at(1 if way == 0 else -1)})

    def zg_wait(way, hop):
        e = hop + 1 if way == 0 else 7 - hop
        arrived(zg_ref(e, way, hop), zg_sems, (way, hop,),
                {"tp": z_at(1)})

    def first_second(i):
        return ((xa, 1), (xb, 3)) if i % 2 == 0 else ((xb, 3), (xa, 1))

    def xg_one(i):
        e = IN_ORDER[i]
        (n1, j1), _ = first_second(i)
        send(patch.at[e, 0], patch.at[e, j1], xg_sems, (e, 0,), {"grp": n1})

    def xg_two(i):
        e = IN_ORDER[i]
        (n1, j1), (n2, j2) = first_second(i)
        send(patch.at[e, 0], patch.at[e, j2], xg_sems, (e, 1,), {"grp": n2})
        arrived(patch.at[e, j1], xg_sems, (e, 0,), {"grp": n1})
        send(patch.at[e, j1], patch.at[e, 2], xg_sems, (e, 2,), {"grp": n2})

    def xg_wait(i):
        e = IN_ORDER[i]
        _, (n2, j2) = first_second(i)
        arrived(patch.at[e, j2], xg_sems, (e, 1,), {"grp": n2})
        arrived(patch.at[e, 2], xg_sems, (e, 2,), {"grp": n2})

    zg_go(0, 0)
    zg_go(1, 0)
    xg_one(0)
    y_step(1)
    zg_wait(0, 0)
    zg_go(0, 1)
    xg_one(1)
    zg_wait(1, 0)
    zg_go(1, 1)
    xg_one(2)
    xg_two(0)

    total = dr_half[:, units(0)].astype(F32)
    for q in (1, 7, 2, 6, 3, 5, 4):
        arrived(dr_in.at[q], dy_sems, (q,), {"seq": slot(q)})
        total = total + dr_in[q].astype(F32)
    dr[mine, units(0)] = total.astype(BF16)
    for q in (4, 3, 5, 2, 6, 1, 7):
        ref = dr.at[mine, units(0)]
        send(ref, ref, dg_sems, (q,), {"seq": slot(q)})

    zg_wait(0, 1)
    zg_go(0, 2)
    xg_one(3)
    zg_wait(1, 1)
    zg_go(1, 2)
    xg_one(4)
    xg_two(1)
    xg_two(2)
    y_step(2)
    zg_wait(0, 2)
    zg_go(0, 3)
    xg_one(5)
    zg_wait(1, 2)
    zg_go(1, 3)
    xg_one(6)
    xg_two(3)
    xg_two(4)
    zg_wait(0, 3)
    zg_wait(1, 3)
    xg_one(7)
    xg_two(5)
    xg_two(6)
    y_step(3)
    for q in (1, 7, 2, 6, 3, 5, 4):
        arrived(dr.at[mine, units(-q)], dg_sems, (q,), {"seq": slot(q)})
    send(dr.at[mine], dr.at[mine], dh_sems, (0,), {"seq": sib})
    xg_two(7)
    sib_wait()

    squares = jnp.zeros((256, 1), F32)
    returned = jnp.zeros((64, 128), F32)
    for i in range(8):
        e = IN_ORDER[i]
        xg_wait(i)
        kb = z_at(-e)
        rows = patch[e].reshape(256, 512)
        returned = returned + dot(patch[e, 0], ret[pl.ds(512 * kb, 512)])
        wide = rows.astype(F32)
        squares = squares + jnp.sum(wide * wide, axis=1, keepdims=True)
        for a in (0, 1):
            w = weights[pl.ds(2 * kb, 2), a].reshape(512, 256)
            if i == 0:
                acc[a] = dot(rows, w)
            else:
                acc[a] += dot(rows, w)
    scale = lax.rsqrt(squares * (1.0 / 4096) + EPS)
    gate = acc[0] * scale
    up = acc[1] * scale
    hidden = (gate / (1.0 + jnp.exp(-gate)) * up).astype(BF16)

    arrived(dr.at[pl.ds(4 - 4 * c, 4)], dh_sems, (0,), {"seq": sib})

    def down_one(i):
        for n in (0, 1):
            part[i, n] = dot(hidden, dr[2 * i + n]).astype(BF16).reshape(4, 64, 128)
        (n1, j1), _ = first_second(i)
        src = part.at[i, :, pl.ds(1 if j1 == 1 else 2, 2)]
        send(src, half_in.at[i], h_sems, (i,), {"grp": n1})

    def down_two(i):
        (n1, j1), (n2, j2) = first_second(i)
        arrived(half_in.at[i], h_sems, (i,), {"grp": n1})
        row = 1 if j1 == 1 else 0
        pair_out[i] = (part[i, :, j2].astype(F32) + half_in[i, :, row].astype(F32)).astype(BF16)
        send(pair_out.at[i], pair_in.at[i], p_sems, (i,), {"grp": n2})

    def down_three(i):
        (n1, j1), (n2, j2) = first_second(i)
        arrived(pair_in.at[i], p_sems, (i,), {"grp": n2})
        row = 0 if j1 == 1 else 1
        for n in (0, 1):
            total = part[i, n, 0].astype(F32) + half_in[i, n, row].astype(F32)
            total = total + pair_in[i, n].astype(F32)
            d = 2 * i + n
            if d == 0:
                own_total.append(total)
            else:
                back_out[d] = total.astype(BF16)
                send(back_out.at[d], back_in.at[d], b_sems, (d,), {"tp": z_at(-d)})

    own_total = []
    order = (2, 1, 3, 0)
    for i in order:
        down_one(i)
    for n in range(5):
        if n < 4:
            down_two(order[n])
        if n > 0:
            down_three(order[n - 1])

    returned = returned + own_total[0]
    for d in (1, 7, 2, 6, 3, 5, 4):
        arrived(back_in.at[d], b_sems, (d,), {"tp": z_at(d)})
        returned = returned + back_in[d].astype(F32)
    returned = returned.astype(BF16)

    spread = lax.dot_general(
        onehot.astype(BF16), returned, (((0,), (0,)), ((), ())), preferred_element_type=F32
    )
    mixed = states.astype(F32) + spread
    ones = jnp.ones((8, 128), F32)
    sq_out[...] = lax.dot_general(
        ones, mixed * mixed, (((1,), (1,)), ((), ())),
        precision=lax.Precision.HIGHEST, preferred_element_type=F32,
    )
    for d in (4, 3, 5, 2, 6, 1, 7):
        send(sq_out, sq_in.at[d], q_sems, (d,), {"tp": z_at(d)})
    total = sq_out[...]
    for d in (1, 7, 2, 6, 3, 5, 4):
        arrived(sq_in.at[d], q_sems, (d,), {"tp": z_at(d)})
        total = total + sq_in[d]
    spread_sum = lax.dot_general(
        total, ones * 0.125, (((0,), (0,)), ((), ())),
        precision=lax.Precision.HIGHEST, preferred_element_type=F32,
    )
    out_ref[...] = (mixed * lax.rsqrt(spread_sum * (1.0 / DL) + EPS)).astype(BF16)
    for copy in started:
        copy.wait_send()


def on_device(
    byte_states, patch_map, lift_weight, gate_weight, up_weight, down_weight, return_weight
):
    vmem = pl.BlockSpec(memory_space=pltpu.VMEM)
    hbm = pl.BlockSpec(memory_space=pl.ANY)
    dma = pltpu.SemaphoreType.DMA
    out = pl.pallas_call(
        kernel,
        out_shape=jax.ShapeDtypeStruct((256, 128), BF16),
        in_specs=[vmem, vmem, hbm, hbm, hbm, hbm, hbm],
        out_specs=vmem,
        scratch_shapes=[
            pltpu.VMEM((128, 4096), BF16),
            pltpu.VMEM((16, 2, 256, 256), BF16),
            pltpu.VMEM((8, 64, 512), BF16),
            pltpu.VMEM((8, 64, 512), BF16),
            pltpu.VMEM((8, 4, 64, 512), BF16),
            pltpu.VMEM((2, 256, 256), F32),
            pltpu.VMEM((256, 256), BF16),
            pltpu.VMEM((4096, 128), BF16),
            pltpu.VMEM((8, 256, 128), BF16),
            pltpu.VMEM((8, 256, 128), BF16),
            pltpu.VMEM((4, 256, 128), BF16),
            pltpu.VMEM((4, 256, 128), BF16),
            pltpu.VMEM((8, 4, 32, 128), BF16),
            pltpu.VMEM((8, 256, 128), BF16),
            pltpu.VMEM((4, 2, 4, 64, 128), BF16),
            pltpu.VMEM((4, 2, 2, 64, 128), BF16),
            pltpu.VMEM((4, 2, 64, 128), BF16),
            pltpu.VMEM((4, 2, 64, 128), BF16),
            pltpu.VMEM((8, 64, 128), BF16),
            pltpu.VMEM((8, 64, 128), BF16),
            pltpu.VMEM((8, 256), F32),
            pltpu.VMEM((8, 8, 256), F32),
            dma((5,)),
            dma((2, 4)), dma((2, 4)),
            dma((8,)), dma((8,)),
            dma((8,)), dma((8,)),
            dma((2, 4)), dma((2, 4)),
            dma((8, 3)), dma((8, 3)),
            dma((8,)), dma((8,)),
            dma((4,)), dma((4,)),
            dma((1,)), dma((1,)),
            dma((8,)), dma((8,)),
            dma((8,)), dma((8,)),
            dma((1,)), dma((1,)),
            dma((4,)), dma((4,)),
            dma((4,)), dma((4,)),
            dma((8,)), dma((8,)),
            dma((8,)), dma((8,)),
        ],
        compiler_params=pltpu.CompilerParams(
            collective_id=0, has_side_effects=True, vmem_limit_bytes=64 * 1024 * 1024
        ),
    )(byte_states[0], patch_map, lift_weight, gate_weight, up_weight, down_weight, return_weight)
    return out[None]


def solution(mesh):
    placed = (
        P("grp", "seq", "tp"),
        P("grp", "seq"),
        P("tp", None),
        P("seq", ("grp", "tp")),
        P("seq", ("grp", "tp")),
        P(("grp", "tp"), "seq"),
        P(None, "tp"),
    )
    return jax.shard_map(
        on_device, mesh=mesh, in_specs=placed, out_specs=P("grp", "seq", "tp"), check_vma=False
    )
```

```python
import jax
import jax.numpy as jnp
from jax import lax
from jax.experimental import pallas as pl
from jax.experimental.pallas import tpu as pltpu
from jax.sharding import PartitionSpec as P

DL = 1024
NMAX = 64
EPS = 1e-05
MESH = pl.DeviceIdType.MESH
F32 = jnp.float32
BF16 = jnp.bfloat16
IN_ORDER = (0, 1, 7, 2, 6, 3, 5, 4)


def dot(a, b):
    return jnp.dot(a, b, preferred_element_type=F32)


def kernel(
    states_hbm, map_hbm, lift_hbm, gate_hbm, up_hbm, down_hbm, ret_hbm, out_ref,
    slots, states_vmem, onehot_t, lift, weights, lift_out, lift_sum, lift_in, patch, acc,
    down, ret, ret_rows, dr_half, dr_in, dr, part, half_in, pair_out, pair_in, back_out, back_in, sq_out, sq_in,
    load_sem,
    y_sends, y_recvs,
    sib_sends, sib_recvs,
    lift_sends, lift_recvs,
    za_sends, za_recvs,
    xg_sends, xg_recvs,
    rz_sends, rz_recvs,
    rx_sends, rx_recvs,
    dn_sends, dn_recvs,
    dy_sends, dy_recvs,
    dg_sends, dg_recvs,
    dh_sends, dh_recvs,
    h_sends, h_recvs,
    p_sends, p_recvs,
    b_sends, b_recvs,
    q_sends, q_recvs,
):
    x = lax.axis_index("grp")
    s = lax.axis_index("seq")
    z = lax.axis_index("tp")
    y = s // 2
    c = s % 2
    xa = x + 1 - 2 * (x % 2)
    xb = 3 - x
    sib = 2 * y + 1 - c
    started = []
    y_sems = (y_sends, y_recvs)
    sib_sems = (sib_sends, sib_recvs)
    lift_sems = (lift_sends, lift_recvs)
    za_sems = (za_sends, za_recvs)
    xg_sems = (xg_sends, xg_recvs)
    rz_sems = (rz_sends, rz_recvs)
    rx_sems = (rx_sends, rx_recvs)
    dn_sems = (dn_sends, dn_recvs)
    dy_sems = (dy_sends, dy_recvs)
    dg_sems = (dg_sends, dg_recvs)
    dh_sems = (dh_sends, dh_recvs)
    h_sems = (h_sends, h_recvs)
    p_sems = (p_sends, p_recvs)
    b_sems = (b_sends, b_recvs)
    q_sems = (q_sends, q_recvs)

    def z_at(d):
        return (z + d + 8) % 8

    def slot(q):
        return 2 * ((y + q + 8) % 8) + c

    def remote(src, dst, sems, index, device):
        return pltpu.make_async_remote_copy(
            src_ref=src, dst_ref=dst, send_sem=sems[0].at[index], recv_sem=sems[1].at[index],
            device_id=device, device_id_type=MESH,
        )

    def send(src, dst, sems, index, device):
        copy = remote(src, dst, sems, index, device)
        copy.start()
        started.append(copy)

    def arrived(ref, sems, index, device):
        remote(ref, ref, sems, index, device).wait_recv()

    loads = [
        pltpu.make_async_copy(map_hbm, slots, load_sem.at[0]),
        pltpu.make_async_copy(states_hbm.at[0], states_vmem, load_sem.at[1]),
        pltpu.make_async_copy(lift_hbm, lift, load_sem.at[2]),
        pltpu.make_async_copy(gate_hbm, weights.at[s, 0], load_sem.at[3]),
        pltpu.make_async_copy(up_hbm, weights.at[s, 1], load_sem.at[4]),
        pltpu.make_async_copy(down_hbm, down.at[c], load_sem.at[5]),
        pltpu.make_async_copy(ret_hbm, ret, load_sem.at[6]),
    ]
    for load in loads:
        load.start()
    barrier = pltpu.get_barrier_semaphore()
    partners = [{"seq": slot(d)} for d in range(1, 8)] + [{"seq": sib}]
    partners += [{"grp": xa}, {"grp": xb}, {"grp": (x + 2) % 4}]
    partners += [{"tp": z_at(d)} for d in range(1, 8)]
    for partner in partners:
        pl.semaphore_signal(barrier, inc=1, device_id=partner, device_id_type=MESH)

    pl.semaphore_wait(barrier, len(partners))

    def y_ref(q, way, hop):
        rows = pl.ds(0, 256) if hop < 3 else pl.ds(128 * way, 128)
        return weights.at[slot(q), :, rows]

    def y_go(way, hop):
        device = {"seq": slot(1 if way == 0 else -1)}
        if hop == 0:
            send(gate_hbm, weights.at[s, 0], y_sems, (way, 0), device)
            send(up_hbm, weights.at[s, 1], y_sems, (way, 4), device)
        else:
            ref = y_ref(-hop if way == 0 else hop, way, hop)
            send(ref, ref, y_sems, (way, hop), device)

    def sib_go(q):
        ref = weights.at[slot(q)]
        send(ref, ref, sib_sems, (q % 8,), {"seq": sib})

    def y_step(hop):
        for way in (0, 1):
            q = -(hop + 1) if way == 0 else hop + 1
            if hop == 0:
                arrived(weights.at[slot(q), 0], y_sems, (way, 0), {"seq": slot(1)})
                arrived(weights.at[slot(q), 1], y_sems, (way, 4), {"seq": slot(1)})
            else:
                arrived(y_ref(q, way, hop), y_sems, (way, hop), {"seq": slot(1)})
            if hop < 3:
                y_go(way, hop + 1)
                sib_go(q)
        if hop == 3:
            sib_go(4)

    def sib_wait():
        for k in range(8):
            arrived(weights.at[2 * ((y + k) % 8) + 1 - c], sib_sems, (k,), {"seq": sib})

    for k in (1, 2, 3):
        send(ret_hbm.at[y, :, x], ret_rows.at[k, :, x], rz_sems, (k,), {"tp": z_at(4 * c + k)})

    def across():
        return remote(ret_hbm.at[y, :, x], ret_rows.at[0, :, x], rz_sems, (0,), {"tp": z_at(4)})

    @pl.when(c == 1)
    def _():
        across().start()

    send(down_hbm, down.at[c], dn_sems, (0,), {"seq": sib})
    y_go(0, 0)
    y_go(1, 0)

    for load in loads[:2]:
        load.wait()
    onehot = (lax.broadcasted_iota(jnp.int32, (NMAX, 256), 0) == slots[...]).astype(F32)
    counts = jnp.sum(onehot, axis=1, keepdims=True)
    states = states_vmem[...]
    sums = dot(onehot.astype(BF16), states)
    pooled = (sums / jnp.maximum(counts, 1.0)).astype(BF16)
    loads[2].wait()

    def lift_go(way, hop):
        device = {"tp": z_at(1 if way == 0 else -1)}
        if hop == 0:
            rows = pl.ds(32 * way, 32)
            send(lift_out.at[4, rows], lift_in.at[way, 0, rows], lift_sems, (way, 0), device)
        else:
            send(lift_sum.at[way, hop], lift_in.at[way, hop], lift_sems, (way, hop), device)

    def lift_arrived(way, hop):
        rows = pl.ds(32 * way, 32) if hop == 0 else pl.ds(0, 64)
        arrived(lift_in.at[way, hop, rows], lift_sems, (way, hop), {"tp": z_at(1)})

    def lift_step(hop):
        for way in (0, 1):
            lift_arrived(way, hop)
            d = 3 - hop if way == 0 else 5 + hop
            if hop == 0:
                rows = pl.ds(32 * way, 32)
                rest = pl.ds(32 * (1 - way), 32)
                lift_sum[way, 1, rest] = lift_out[d, rest]
                lift_sum[way, 1, rows] = (
                    lift_out[d, rows].astype(F32) + lift_in[way, 0, rows].astype(F32)
                ).astype(BF16)
            else:
                lift_sum[way, hop + 1] = (
                    lift_out[d].astype(F32) + lift_in[way, hop].astype(F32)
                ).astype(BF16)
            lift_go(way, hop + 1)

    for d in (4, 3, 5, 2, 6, 1, 7, 0):
        columns = lift[:, pl.ds(pl.multiple_of(512 * z_at(d), 512), 512)]
        lift_out[d] = dot(pooled, columns).astype(BF16)
        if d == 4:
            lift_go(0, 0)
            lift_go(1, 0)
    onehot_t[...] = jnp.transpose(onehot).astype(BF16)
    for load in loads[3:]:
        load.wait()
    sib_go(0)

    @pl.when(c == 0)
    def _():
        ret_rows[0, :, x] = ret[y, :, x]

    def ret_x():
        for k in (1, 2, 3):
            arrived(ret_rows.at[k, :, x], rz_sems, (k,), {"tp": z_at(1)})

        @pl.when(c == 1)
        def _():
            across().wait_recv()

        for j in (2, 1, 3):
            ref = ret_rows.at[:, :, x]
            send(ref, ref, rx_sems, (j,), {"grp": (x + j) % 4})

    mine = pl.ds(4 * c, 4)

    def units(q):
        return pl.ds(32 * ((y + q + 8) % 8), 32)

    def dr_products():
        for j in (1, 3, 2):
            arrived(ret_rows.at[:, :, x], rx_sems, (j,), {"grp": xa})
        arrived(down.at[1 - c], dn_sems, (0,), {"seq": sib})
        for k in range(4):
            val = dot(down[0], ret_rows[k, 0].reshape(256, 128))
            val = val + dot(down[1], ret_rows[k, 1].reshape(256, 128))
            dr_half[k] = val.astype(BF16)
        for q in (4, 3, 5, 2, 6, 1, 7):
            send(dr_half.at[:, units(q)], dr_in.at[q], dy_sems, (q,), {"seq": slot(q)})

    def dr_total():
        total = dr_half[:, units(0)].astype(F32)
        for q in (1, 7, 2, 6, 3, 5, 4):
            arrived(dr_in.at[q], dy_sems, (q,), {"seq": slot(q)})
            total = total + dr_in[q].astype(F32)
        dr[mine, units(0)] = total.astype(BF16)
        for q in (4, 3, 5, 2, 6, 1, 7):
            ref = dr.at[mine, units(0)]
            send(ref, ref, dg_sems, (q,), {"seq": slot(q)})

    def dr_share():
        for q in (1, 7, 2, 6, 3, 5, 4):
            arrived(dr.at[mine, units(-q)], dg_sems, (q,), {"seq": slot(q)})
        send(dr.at[mine], dr.at[mine], dh_sems, (0,), {"seq": sib})

    def ring_places(way, hop):
        return (hop, hop + 1) if way == 0 else ((8 - hop) % 8, 7 - hop)

    def za_ref(e, way, hop):
        rows = pl.ds(0, 64) if hop < 3 else pl.ds(32 * way, 32)
        return patch.at[e, 0, rows]

    def za_go(way, hop):
        e, e2 = ring_places(way, hop)
        send(za_ref(e, way, hop), za_ref(e2, way, hop), za_sems, (way, hop),
             {"tp": z_at(1 if way == 0 else -1)})

    def first_second(i):
        return ((xa, 1), (xb, 3)) if i % 2 == 0 else ((xb, 3), (xa, 1))

    def xg_one(i):
        e = IN_ORDER[i]
        (n1, j1), _ = first_second(i)
        send(patch.at[e, 0], patch.at[e, j1], xg_sems, (e, 0), {"grp": n1})

    def xg_two(i):
        e = IN_ORDER[i]
        (n1, j1), (n2, j2) = first_second(i)
        send(patch.at[e, 0], patch.at[e, j2], xg_sems, (e, 1), {"grp": n2})
        arrived(patch.at[e, j1], xg_sems, (e, 0), {"grp": n1})
        send(patch.at[e, j1], patch.at[e, 2], xg_sems, (e, 2), {"grp": n2})

    def xg_wait(i):
        e = IN_ORDER[i]
        _, (n2, j2) = first_second(i)
        arrived(patch.at[e, j2], xg_sems, (e, 1), {"grp": n2})
        arrived(patch.at[e, 2], xg_sems, (e, 2), {"grp": n2})

    def za_step(hop):
        for way in (0, 1):
            e2 = ring_places(way, hop)[1]
            arrived(za_ref(e2, way, hop), za_sems, (way, hop), {"tp": z_at(1)})
            if hop < 3:
                za_go(way, hop + 1)
                xg_one(2 * hop + 1 + way)
        if hop == 3:
            xg_one(7)

    def patch_start():
        block = lift_out[0].astype(F32)
        for way in (0, 1):
            lift_arrived(way, 3)
            block = block + lift_in[way, 3].astype(F32)
        patch[0, 0] = block.astype(BF16)
        za_go(0, 0)
        za_go(1, 0)
        xg_one(0)

    lift_step(0)
    ret_x()
    lift_step(1)
    y_step(0)
    lift_step(2)
    dr_products()
    patch_start()
    y_step(1)
    za_step(0)
    xg_two(0)
    za_step(1)
    xg_two(1)
    xg_two(2)
    za_step(2)
    y_step(2)
    xg_two(3)
    xg_two(4)
    za_step(3)
    dr_total()
    xg_two(5)
    xg_two(6)
    y_step(3)
    xg_two(7)

    squares = jnp.zeros((256, 1), F32)
    returned = jnp.zeros((64, 128), F32)

    def multiply(i, squares, returned):
        xg_wait(i)
        e = IN_ORDER[i]
        kb = z_at(-e)
        rows = patch[e].reshape(256, 512)
        returned = returned + dot(patch[e, 0], ret[kb].reshape(512, 128))
        wide = rows.astype(F32)
        squares = squares + jnp.sum(wide * wide, axis=1, keepdims=True)
        for a in (0, 1):
            w = weights[pl.ds(2 * kb, 2), a].reshape(512, 256)
            if i == 0:
                acc[a] = dot(rows, w)
            else:
                acc[a] += dot(rows, w)
        return squares, returned

    sib_wait()
    for i in range(6):
        squares, returned = multiply(i, squares, returned)
    dr_share()
    for i in range(6, 8):
        squares, returned = multiply(i, squares, returned)

    scale = lax.rsqrt(squares * (1.0 / 4096) + EPS)
    gate = acc[0] * scale
    up = acc[1] * scale
    hidden = (gate / (1.0 + jnp.exp(-gate)) * up).astype(BF16)

    arrived(dr.at[pl.ds(4 - 4 * c, 4)], dh_sems, (0,), {"seq": sib})

    def down_one(i):
        for n in (0, 1):
            part[i, n] = dot(hidden, dr[2 * i + n]).astype(BF16).reshape(4, 64, 128)
        (n1, j1), _ = first_second(i)
        src = part.at[i, :, pl.ds(1 if j1 == 1 else 2, 2)]
        send(src, half_in.at[i], h_sems, (i,), {"grp": n1})

    def down_two(i):
        (n1, j1), (n2, j2) = first_second(i)
        arrived(half_in.at[i], h_sems, (i,), {"grp": n1})
        row = 1 if j1 == 1 else 0
        pair_out[i] = (part[i, :, j2].astype(F32) + half_in[i, :, row].astype(F32)).astype(BF16)
        send(pair_out.at[i], pair_in.at[i], p_sems, (i,), {"grp": n2})

    def down_three(i):
        (n1, j1), (n2, j2) = first_second(i)
        arrived(pair_in.at[i], p_sems, (i,), {"grp": n2})
        row = 0 if j1 == 1 else 1
        for n in (0, 1):
            total = part[i, n, 0].astype(F32) + half_in[i, n, row].astype(F32)
            total = total + pair_in[i, n].astype(F32)
            d = 2 * i + n
            if d == 0:
                own_total.append(total)
            else:
                back_out[d] = total.astype(BF16)
                send(back_out.at[d], back_in.at[d], b_sems, (d,), {"tp": z_at(-d)})

    own_total = []
    order = (2, 1, 3, 0)
    for i in order:
        down_one(i)
    for n in range(5):
        if n < 4:
            down_two(order[n])
        if n > 0:
            down_three(order[n - 1])

    returned = returned + own_total[0]
    for d in (1, 7, 2, 6, 3, 5, 4):
        arrived(back_in.at[d], b_sems, (d,), {"tp": z_at(d)})
        returned = returned + back_in[d].astype(F32)
    returned = returned.astype(BF16)

    mixed = states_vmem[...].astype(F32) + dot(onehot_t[...], returned)
    square = mixed * mixed
    upper = square.astype(BF16)
    lower = (square - upper.astype(F32)).astype(BF16)
    ones = jnp.ones((8, 128), BF16)
    dims = (((1,), (1,)), ((), ()))
    sq_out[...] = lax.dot_general(ones, upper, dims, preferred_element_type=F32) + (
        lax.dot_general(ones, lower, dims, preferred_element_type=F32)
    )
    for d in (4, 3, 5, 2, 6, 1, 7):
        send(sq_out, sq_in.at[d], q_sems, (d,), {"tp": z_at(d)})
    total = sq_out[...]
    for d in (1, 7, 2, 6, 3, 5, 4):
        arrived(sq_in.at[d], q_sems, (d,), {"tp": z_at(d)})
        total = total + sq_in[d]
    inverse = lax.rsqrt(total[0:1] * (1.0 / DL) + EPS)
    inverse = jnp.transpose(jnp.broadcast_to(inverse, (128, 256)))
    out_ref[...] = (mixed * inverse).astype(BF16)

    @pl.when(c == 1)
    def _():
        across().wait_send()

    for copy in started:
        copy.wait_send()


def on_device(
    byte_states, patch_map, lift_weight, gate_weight, up_weight, down_weight, return_weight
):
    vmem = pl.BlockSpec(memory_space=pltpu.VMEM)
    hbm = pl.BlockSpec(memory_space=pl.ANY)
    dma = pltpu.SemaphoreType.DMA
    out = pl.pallas_call(
        kernel,
        out_shape=jax.ShapeDtypeStruct((256, 128), BF16),
        in_specs=[hbm] * 7,
        out_specs=vmem,
        scratch_shapes=[
            pltpu.VMEM((1, 256), jnp.int32),
            pltpu.VMEM((256, 128), BF16),
            pltpu.VMEM((256, 64), BF16),
            pltpu.VMEM((128, 4096), BF16),
            pltpu.VMEM((16, 2, 256, 256), BF16),
            pltpu.VMEM((8, 64, 512), BF16),
            pltpu.VMEM((2, 4, 64, 512), BF16),
            pltpu.VMEM((2, 4, 64, 512), BF16),
            pltpu.VMEM((8, 4, 64, 512), BF16),
            pltpu.VMEM((2, 256, 256), F32),
            pltpu.VMEM((2, 256, 256), BF16),
            pltpu.VMEM((8, 2, 4, 64, 128), BF16),
            pltpu.VMEM((4, 2, 4, 64, 128), BF16),
            pltpu.VMEM((4, 256, 128), BF16),
            pltpu.VMEM((8, 4, 32, 128), BF16),
            pltpu.VMEM((8, 256, 128), BF16),
            pltpu.VMEM((4, 2, 4, 64, 128), BF16),
            pltpu.VMEM((4, 2, 2, 64, 128), BF16),
            pltpu.VMEM((4, 2, 64, 128), BF16),
            pltpu.VMEM((4, 2, 64, 128), BF16),
            pltpu.VMEM((8, 64, 128), BF16),
            pltpu.VMEM((8, 64, 128), BF16),
            pltpu.VMEM((8, 256), F32),
            pltpu.VMEM((8, 8, 256), F32),
            dma((7,)),
            dma((2, 5)), dma((2, 5)),
            dma((8,)), dma((8,)),
            dma((2, 4)), dma((2, 4)),
            dma((2, 4)), dma((2, 4)),
            dma((8, 3)), dma((8, 3)),
            dma((4,)), dma((4,)),
            dma((4,)), dma((4,)),
            dma((1,)), dma((1,)),
            dma((8,)), dma((8,)),
            dma((8,)), dma((8,)),
            dma((1,)), dma((1,)),
            dma((4,)), dma((4,)),
            dma((4,)), dma((4,)),
            dma((8,)), dma((8,)),
            dma((8,)), dma((8,)),
        ],
        compiler_params=pltpu.CompilerParams(
            collective_id=0, has_side_effects=True, vmem_limit_bytes=64 * 1024 * 1024
        ),
    )(
        byte_states, patch_map, lift_weight, gate_weight, up_weight, down_weight,
        return_weight.reshape(8, 2, 4, 64, 128),
    )
    return out[None]


def solution(mesh):
    placed = (
        P("grp", "seq", "tp"),
        P("grp", "seq"),
        P("tp", None),
        P("seq", ("grp", "tp")),
        P("seq", ("grp", "tp")),
        P(("grp", "tp"), "seq"),
        P(None, "tp"),
    )
    return jax.shard_map(
        on_device, mesh=mesh, in_specs=placed, out_specs=P("grp", "seq", "tp"), check_vma=False
    )
```

```python
import jax
import jax.numpy as jnp
from jax import lax
from jax.experimental import pallas as pl
from jax.experimental.pallas import tpu as pltpu
from jax.sharding import PartitionSpec as P

DL = 1024
NMAX = 64
EPS = 1e-05
MESH = pl.DeviceIdType.MESH
F32 = jnp.float32
BF16 = jnp.bfloat16
IN_ORDER = (0, 1, 7, 2, 6, 3, 5, 4)


def dot(a, b):
    return jnp.dot(a, b, preferred_element_type=F32)


def kernel(
    states_hbm, map_hbm, lift_hbm, gate_hbm, up_hbm, down_hbm, ret_hbm, out_ref,
    slots, states_vmem, onehot_t, lift, weights, lift_out, lift_far, lift_sum, lift_in, patch, acc,
    down, ret, ret_rows, dr_half, dr_in, dr, part, part_in, back_out, back_in, sq_out, sq_in,
    load_sem,
    y_sends, y_recvs,
    sib_sends, sib_recvs,
    lift_sends, lift_recvs,
    za_sends, za_recvs,
    xg_sends, xg_recvs,
    rz_sends, rz_recvs,
    rx_sends, rx_recvs,
    dn_sends, dn_recvs,
    dy_sends, dy_recvs,
    dg_sends, dg_recvs,
    dh_sends, dh_recvs,
    h_sends, h_recvs,
    b_sends, b_recvs,
    q_sends, q_recvs,
):
    x = lax.axis_index("grp")
    s = lax.axis_index("seq")
    z = lax.axis_index("tp")
    y = s // 2
    c = s % 2
    xa = x + 1 - 2 * (x % 2)
    xb = 3 - x
    sib = 2 * y + 1 - c
    started = []
    y_sems = (y_sends, y_recvs)
    sib_sems = (sib_sends, sib_recvs)
    lift_sems = (lift_sends, lift_recvs)
    za_sems = (za_sends, za_recvs)
    xg_sems = (xg_sends, xg_recvs)
    rz_sems = (rz_sends, rz_recvs)
    rx_sems = (rx_sends, rx_recvs)
    dn_sems = (dn_sends, dn_recvs)
    dy_sems = (dy_sends, dy_recvs)
    dg_sems = (dg_sends, dg_recvs)
    dh_sems = (dh_sends, dh_recvs)
    h_sems = (h_sends, h_recvs)
    b_sems = (b_sends, b_recvs)
    q_sems = (q_sends, q_recvs)

    def z_at(d):
        return (z + d + 8) % 8

    def slot(q):
        return 2 * ((y + q + 8) % 8) + c

    def remote(src, dst, sems, index, device):
        return pltpu.make_async_remote_copy(
            src_ref=src, dst_ref=dst, send_sem=sems[0].at[index], recv_sem=sems[1].at[index],
            device_id=device, device_id_type=MESH,
        )

    def send(src, dst, sems, index, device):
        copy = remote(src, dst, sems, index, device)
        copy.start()
        started.append(copy)

    def arrived(ref, sems, index, device):
        remote(ref, ref, sems, index, device).wait_recv()

    loads = [
        pltpu.make_async_copy(map_hbm, slots, load_sem.at[0]),
        pltpu.make_async_copy(states_hbm.at[0], states_vmem, load_sem.at[1]),
        pltpu.make_async_copy(lift_hbm, lift, load_sem.at[2]),
        pltpu.make_async_copy(gate_hbm, weights.at[s, 0], load_sem.at[3]),
        pltpu.make_async_copy(up_hbm, weights.at[s, 1], load_sem.at[4]),
        pltpu.make_async_copy(down_hbm, down.at[c], load_sem.at[5]),
        pltpu.make_async_copy(ret_hbm, ret, load_sem.at[6]),
    ]
    for load in loads:
        load.start()
    barrier = pltpu.get_barrier_semaphore()
    partners = [{"seq": slot(d)} for d in range(1, 8)] + [{"seq": sib}]
    partners += [{"grp": xa}, {"grp": xb}, {"grp": (x + 2) % 4}]
    partners += [{"tp": z_at(d)} for d in range(1, 8)]
    for partner in partners:
        pl.semaphore_signal(barrier, inc=1, device_id=partner, device_id_type=MESH)

    pl.semaphore_wait(barrier, len(partners))

    def y_ref(q, way, hop):
        rows = pl.ds(0, 256) if hop < 3 else pl.ds(128 * way, 128)
        return weights.at[slot(q), :, rows]

    def y_go(way, hop):
        device = {"seq": slot(1 if way == 0 else -1)}
        if hop == 0:
            send(gate_hbm, weights.at[s, 0], y_sems, (way, 0), device)
            send(up_hbm, weights.at[s, 1], y_sems, (way, 4), device)
        else:
            ref = y_ref(-hop if way == 0 else hop, way, hop)
            send(ref, ref, y_sems, (way, hop), device)

    def sib_go(q):
        ref = weights.at[slot(q)]
        send(ref, ref, sib_sems, (q % 8,), {"seq": sib})

    def y_step(hop):
        for way in (0, 1):
            q = -(hop + 1) if way == 0 else hop + 1
            if hop == 0:
                arrived(weights.at[slot(q), 0], y_sems, (way, 0), {"seq": slot(1)})
                arrived(weights.at[slot(q), 1], y_sems, (way, 4), {"seq": slot(1)})
            else:
                arrived(y_ref(q, way, hop), y_sems, (way, hop), {"seq": slot(1)})
            if hop < 3:
                y_go(way, hop + 1)
                sib_go(q)
        if hop == 3:
            sib_go(4)

    def sib_wait():
        for k in range(8):
            arrived(weights.at[2 * ((y + k) % 8) + 1 - c], sib_sems, (k,), {"seq": sib})

    for k in (1, 2, 3):
        send(ret_hbm.at[y, :, x], ret_rows.at[k, :, x], rz_sems, (k,), {"tp": z_at(4 * c + k)})

    def across():
        return remote(ret_hbm.at[y, :, x], ret_rows.at[0, :, x], rz_sems, (0,), {"tp": z_at(4)})

    @pl.when(c == 1)
    def _():
        across().start()

    send(down_hbm, down.at[c], dn_sems, (0,), {"seq": sib})
    y_go(0, 0)
    y_go(1, 0)

    for load in loads[:2]:
        load.wait()
    onehot = (lax.broadcasted_iota(jnp.int32, (NMAX, 256), 0) == slots[...]).astype(F32)
    counts = jnp.sum(onehot, axis=1, keepdims=True)
    states = states_vmem[...]
    sums = dot(onehot.astype(BF16), states)
    pooled = (sums / jnp.maximum(counts, 1.0)).astype(BF16)
    loads[2].wait()

    def toward(way, d):
        return {"tp": z_at(d if way == 0 else -d)}

    def lift_go(way):
        sign = 1 if way == 0 else -1
        rows = pl.ds(32 * way, 32)
        send(lift_out.at[4, rows], lift_far.at[way], lift_sems, (way, 0), toward(way, 2))
        send(lift_out.at[3 * sign % 8], lift_in.at[way, 0], lift_sems, (way, 1), toward(way, 1))

    def lift_near(way):
        sign = 1 if way == 0 else -1
        send(lift_out.at[sign % 8], lift_in.at[way, 1], lift_sems, (way, 2), toward(way, 1))

    def lift_mid():
        for way in (0, 1):
            sign = 1 if way == 0 else -1
            arrived(lift_far.at[way], lift_sems, (way, 0), toward(way, 2))
            arrived(lift_in.at[way, 0], lift_sems, (way, 1), toward(way, 1))
            total = lift_out[2 * sign % 8].astype(F32) + lift_in[way, 0].astype(F32)
            far = lift_far[way].astype(F32)
            zero = jnp.zeros((32, 512), F32)
            far = jnp.concatenate([far, zero] if way == 0 else [zero, far], axis=0)
            lift_sum[way] = (total + far).astype(BF16)
            send(lift_sum.at[way], lift_in.at[way, 2], lift_sems, (way, 3), toward(way, 2))

    for d in (4, 3, 5, 1, 7, 2, 6, 0):
        columns = lift[:, pl.ds(pl.multiple_of(512 * z_at(d), 512), 512)]
        lift_out[d] = dot(pooled, columns).astype(BF16)
        if d == 5:
            lift_go(0)
            lift_go(1)
        if d == 7:
            lift_near(0)
            lift_near(1)
    onehot_t[...] = jnp.transpose(onehot).astype(BF16)
    for load in loads[3:]:
        load.wait()
    sib_go(0)

    @pl.when(c == 0)
    def _():
        ret_rows[0, :, x] = ret[y, :, x]

    def ret_x():
        for k in (1, 2, 3):
            arrived(ret_rows.at[k, :, x], rz_sems, (k,), {"tp": z_at(1)})

        @pl.when(c == 1)
        def _():
            across().wait_recv()

        for j in (2, 1, 3):
            ref = ret_rows.at[:, :, x]
            send(ref, ref, rx_sems, (j,), {"grp": (x + j) % 4})

    mine = pl.ds(4 * c, 4)

    def units(q):
        return pl.ds(32 * ((y + q + 8) % 8), 32)

    def dr_products():
        for j in (1, 3, 2):
            arrived(ret_rows.at[:, :, x], rx_sems, (j,), {"grp": xa})
        arrived(down.at[1 - c], dn_sems, (0,), {"seq": sib})
        for k in range(4):
            val = dot(down[0], ret_rows[k, 0].reshape(256, 128))
            val = val + dot(down[1], ret_rows[k, 1].reshape(256, 128))
            dr_half[k] = val.astype(BF16)
        for q in (4, 3, 5, 2, 6, 1, 7):
            send(dr_half.at[:, units(q)], dr_in.at[q], dy_sems, (q,), {"seq": slot(q)})

    def dr_total():
        total = dr_half[:, units(0)].astype(F32)
        for q in (1, 7, 2, 6, 3, 5, 4):
            arrived(dr_in.at[q], dy_sems, (q,), {"seq": slot(q)})
            total = total + dr_in[q].astype(F32)
        dr[mine, units(0)] = total.astype(BF16)
        for q in (4, 3, 5, 2, 6, 1, 7):
            ref = dr.at[mine, units(0)]
            send(ref, ref, dg_sems, (q,), {"seq": slot(q)})

    def dr_share():
        for q in (1, 7, 2, 6, 3, 5, 4):
            arrived(dr.at[mine, units(-q)], dg_sems, (q,), {"seq": slot(q)})
        send(dr.at[mine], dr.at[mine], dh_sems, (0,), {"seq": sib})

    def first_second(i):
        return ((xa, 1), (xb, 3)) if i % 2 == 0 else ((xb, 3), (xa, 1))

    def xg_one(i):
        e = IN_ORDER[i]
        (n1, j1), _ = first_second(i)
        send(patch.at[e, 0], patch.at[e, j1], xg_sems, (e, 0), {"grp": n1})

    def xg_two(i):
        e = IN_ORDER[i]
        (n1, j1), (n2, j2) = first_second(i)
        send(patch.at[e, 0], patch.at[e, j2], xg_sems, (e, 1), {"grp": n2})
        arrived(patch.at[e, j1], xg_sems, (e, 0), {"grp": n1})
        send(patch.at[e, j1], patch.at[e, 2], xg_sems, (e, 2), {"grp": n2})

    def xg_wait(i):
        e = IN_ORDER[i]
        _, (n2, j2) = first_second(i)
        arrived(patch.at[e, j2], xg_sems, (e, 1), {"grp": n2})
        arrived(patch.at[e, 2], xg_sems, (e, 2), {"grp": n2})

    def za_near():
        for way in (0, 1):
            e = 1 if way == 0 else 7
            arrived(patch.at[e, 0], za_sems, (way, 0), toward(way, 1))
            xg_one(1 + way)

    def za_mid():
        for way in (0, 1):
            e, e3 = ((2, 3), (6, 5))[way]
            rows = pl.ds(32 * way, 32)
            arrived(patch.at[e, 0], za_sems, (way, 1), toward(way, 2))
            send(patch.at[e, 0, rows], patch.at[4, 0, rows], za_sems, (way, 3), toward(way, 2))
            send(patch.at[e, 0], patch.at[e3, 0], za_sems, (way, 2), toward(way, 1))
            xg_one(3 + way)

    def za_far():
        for way in (0, 1):
            arrived(patch.at[3 if way == 0 else 5, 0], za_sems, (way, 2), toward(way, 1))
            xg_one(5 + way)
        for way in (0, 1):
            rows = pl.ds(32 * way, 32)
            arrived(patch.at[4, 0, rows], za_sems, (way, 3), toward(way, 2))
        xg_one(7)

    def patch_start():
        block = lift_out[0].astype(F32)
        for way in (0, 1):
            arrived(lift_in.at[way, 1], lift_sems, (way, 2), toward(way, 1))
            arrived(lift_in.at[way, 2], lift_sems, (way, 3), toward(way, 2))
            block = block + lift_in[way, 1].astype(F32) + lift_in[way, 2].astype(F32)
        patch[0, 0] = block.astype(BF16)
        for way in (0, 1):
            for d in (2, 1):
                e = d if way == 0 else 8 - d
                send(patch.at[0, 0], patch.at[e, 0], za_sems, (way, d - 1), toward(way, d))
        xg_one(0)

    ret_x()
    lift_mid()
    y_step(0)
    patch_start()
    dr_products()
    za_near()
    za_mid()
    xg_two(0)
    y_step(1)
    xg_two(1)
    xg_two(2)
    za_far()
    xg_two(3)
    xg_two(4)
    dr_total()
    y_step(2)
    xg_two(5)
    xg_two(6)
    xg_two(7)
    dr_share()
    y_step(3)

    squares = jnp.zeros((256, 1), F32)
    returned = jnp.zeros((64, 128), F32)

    def multiply(i, squares, returned):
        xg_wait(i)
        e = IN_ORDER[i]
        kb = z_at(-e)
        rows = patch[e].reshape(256, 512)
        returned = returned + dot(patch[e, 0], ret[kb].reshape(512, 128))
        wide = rows.astype(F32)
        squares = squares + jnp.sum(wide * wide, axis=1, keepdims=True)
        for a in (0, 1):
            w = weights[pl.ds(2 * kb, 2), a].reshape(512, 256)
            if i == 0:
                acc[a] = dot(rows, w)
            else:
                acc[a] += dot(rows, w)
        return squares, returned

    sib_wait()
    for i in range(8):
        squares, returned = multiply(i, squares, returned)

    scale = lax.rsqrt(squares * (1.0 / 4096) + EPS)
    gate = acc[0] * scale
    up = acc[1] * scale
    hidden = (gate / (1.0 + jnp.exp(-gate)) * up).astype(BF16)

    arrived(dr.at[pl.ds(4 - 4 * c, 4)], dh_sems, (0,), {"seq": sib})

    def down_one(i):
        for n in (0, 1):
            part[i, :, n] = dot(hidden, dr[2 * i + n]).astype(BF16).reshape(4, 64, 128)
        for j, n in ((2, (x + 2) % 4), (1, xa), (3, xb)):
            send(part.at[i, j], part_in.at[i, j], h_sems, (i, j), {"grp": n})

    def down_two(i):
        total = part[i, 0].astype(F32)
        for j in (1, 3, 2):
            arrived(part_in.at[i, j], h_sems, (i, j), {"grp": xa})
            total = total + part_in[i, j].astype(F32)
        for n in (0, 1):
            d = 2 * i + n
            if d == 0:
                own_total.append(total[n])
            else:
                back_out[d] = total[n].astype(BF16)
                send(back_out.at[d], back_in.at[d], b_sems, (d,), {"tp": z_at(-d)})

    own_total = []
    order = (2, 1, 3, 0)
    for i in order:
        down_one(i)
    for i in order:
        down_two(i)

    returned = returned + own_total[0]
    for d in (1, 7, 2, 6, 3, 5, 4):
        arrived(back_in.at[d], b_sems, (d,), {"tp": z_at(d)})
        returned = returned + back_in[d].astype(F32)
    returned = returned.astype(BF16)

    mixed = states_vmem[...].astype(F32) + dot(onehot_t[...], returned)
    square = mixed * mixed
    upper = square.astype(BF16)
    lower = (square - upper.astype(F32)).astype(BF16)
    ones = jnp.ones((8, 128), BF16)
    dims = (((1,), (1,)), ((), ()))
    sq_out[...] = lax.dot_general(ones, upper, dims, preferred_element_type=F32) + (
        lax.dot_general(ones, lower, dims, preferred_element_type=F32)
    )
    for d in (4, 3, 5, 2, 6, 1, 7):
        send(sq_out, sq_in.at[d], q_sems, (d,), {"tp": z_at(d)})
    total = sq_out[...]
    for d in (1, 7, 2, 6, 3, 5, 4):
        arrived(sq_in.at[d], q_sems, (d,), {"tp": z_at(d)})
        total = total + sq_in[d]
    inverse = lax.rsqrt(total[0:1] * (1.0 / DL) + EPS)
    inverse = jnp.transpose(jnp.broadcast_to(inverse, (128, 256)))
    out_ref[...] = (mixed * inverse).astype(BF16)

    @pl.when(c == 1)
    def _():
        across().wait_send()

    for copy in started:
        copy.wait_send()


def on_device(
    byte_states, patch_map, lift_weight, gate_weight, up_weight, down_weight, return_weight
):
    vmem = pl.BlockSpec(memory_space=pltpu.VMEM)
    hbm = pl.BlockSpec(memory_space=pl.ANY)
    dma = pltpu.SemaphoreType.DMA
    out = pl.pallas_call(
        kernel,
        out_shape=jax.ShapeDtypeStruct((256, 128), BF16),
        in_specs=[hbm] * 7,
        out_specs=vmem,
        scratch_shapes=[
            pltpu.VMEM((1, 256), jnp.int32),
            pltpu.VMEM((256, 128), BF16),
            pltpu.VMEM((256, 64), BF16),
            pltpu.VMEM((128, 4096), BF16),
            pltpu.VMEM((16, 2, 256, 256), BF16),
            pltpu.VMEM((8, 64, 512), BF16),
            pltpu.VMEM((2, 32, 512), BF16),
            pltpu.VMEM((2, 64, 512), BF16),
            pltpu.VMEM((2, 3, 64, 512), BF16),
            pltpu.VMEM((8, 4, 64, 512), BF16),
            pltpu.VMEM((2, 256, 256), F32),
            pltpu.VMEM((2, 256, 256), BF16),
            pltpu.VMEM((8, 2, 4, 64, 128), BF16),
            pltpu.VMEM((4, 2, 4, 64, 128), BF16),
            pltpu.VMEM((4, 256, 128), BF16),
            pltpu.VMEM((8, 4, 32, 128), BF16),
            pltpu.VMEM((8, 256, 128), BF16),
            pltpu.VMEM((4, 4, 2, 64, 128), BF16),
            pltpu.VMEM((4, 4, 2, 64, 128), BF16),
            pltpu.VMEM((8, 64, 128), BF16),
            pltpu.VMEM((8, 64, 128), BF16),
            pltpu.VMEM((8, 256), F32),
            pltpu.VMEM((8, 8, 256), F32),
            dma((7,)),
            dma((2, 5)), dma((2, 5)),
            dma((8,)), dma((8,)),
            dma((2, 4)), dma((2, 4)),
            dma((2, 4)), dma((2, 4)),
            dma((8, 3)), dma((8, 3)),
            dma((4,)), dma((4,)),
            dma((4,)), dma((4,)),
            dma((1,)), dma((1,)),
            dma((8,)), dma((8,)),
            dma((8,)), dma((8,)),
            dma((1,)), dma((1,)),
            dma((4, 4)), dma((4, 4)),
            dma((8,)), dma((8,)),
            dma((8,)), dma((8,)),
        ],
        compiler_params=pltpu.CompilerParams(
            collective_id=0, has_side_effects=True, vmem_limit_bytes=64 * 1024 * 1024
        ),
    )(
        byte_states, patch_map, lift_weight, gate_weight, up_weight, down_weight,
        return_weight.reshape(8, 2, 4, 64, 128),
    )
    return out[None]


def solution(mesh):
    placed = (
        P("grp", "seq", "tp"),
        P("grp", "seq"),
        P("tp", None),
        P("seq", ("grp", "tp")),
        P("seq", ("grp", "tp")),
        P(("grp", "tp"), "seq"),
        P(None, "tp"),
    )
    return jax.shard_map(
        on_device, mesh=mesh, in_specs=placed, out_specs=P("grp", "seq", "tp"), check_vma=False
    )
```

```python
import jax
import jax.numpy as jnp
from jax import lax
from jax.experimental import pallas as pl
from jax.experimental.pallas import tpu as pltpu
from jax.sharding import PartitionSpec as P

DL = 1024
NMAX = 64
EPS = 1e-05
MESH = pl.DeviceIdType.MESH
F32 = jnp.float32
BF16 = jnp.bfloat16
IN_ORDER = (0, 1, 7, 2, 6, 3, 5, 4)


def dot(a, b):
    return jnp.dot(a, b, preferred_element_type=F32)


def kernel(
    states_hbm, map_hbm, lift_hbm, gate_hbm, up_hbm, down_hbm, ret_hbm, out_ref,
    slots, states_vmem, onehot_t, lift, weights, lift_out, lift_far, lift_sum, lift_in, patch, acc,
    down, ret, ret_rows, dr_half, dr_far, dr_sum, dr_in, dr, part, part_in, back_out, back_in, sq_out, sq_in,
    load_sem,
    y_sends, y_recvs,
    sib_sends, sib_recvs,
    lift_sends, lift_recvs,
    za_sends, za_recvs,
    xg_sends, xg_recvs,
    rz_sends, rz_recvs,
    rx_sends, rx_recvs,
    dn_sends, dn_recvs,
    dy_sends, dy_recvs,
    dg_sends, dg_recvs,
    dh_sends, dh_recvs,
    h_sends, h_recvs,
    b_sends, b_recvs,
    q_sends, q_recvs,
):
    x = lax.axis_index("grp")
    s = lax.axis_index("seq")
    z = lax.axis_index("tp")
    y = s // 2
    c = s % 2
    xa = x + 1 - 2 * (x % 2)
    xb = 3 - x
    sib = 2 * y + 1 - c
    started = []
    y_sems = (y_sends, y_recvs)
    sib_sems = (sib_sends, sib_recvs)
    lift_sems = (lift_sends, lift_recvs)
    za_sems = (za_sends, za_recvs)
    xg_sems = (xg_sends, xg_recvs)
    rz_sems = (rz_sends, rz_recvs)
    rx_sems = (rx_sends, rx_recvs)
    dn_sems = (dn_sends, dn_recvs)
    dy_sems = (dy_sends, dy_recvs)
    dg_sems = (dg_sends, dg_recvs)
    dh_sems = (dh_sends, dh_recvs)
    h_sems = (h_sends, h_recvs)
    b_sems = (b_sends, b_recvs)
    q_sems = (q_sends, q_recvs)

    def z_at(d):
        return (z + d + 8) % 8

    def slot(q):
        return 2 * ((y + q + 8) % 8) + c

    def remote(src, dst, sems, index, device):
        return pltpu.make_async_remote_copy(
            src_ref=src, dst_ref=dst, send_sem=sems[0].at[index], recv_sem=sems[1].at[index],
            device_id=device, device_id_type=MESH,
        )

    def send(src, dst, sems, index, device):
        copy = remote(src, dst, sems, index, device)
        copy.start()
        started.append(copy)

    def arrived(ref, sems, index, device):
        remote(ref, ref, sems, index, device).wait_recv()

    loads = [
        pltpu.make_async_copy(map_hbm, slots, load_sem.at[0]),
        pltpu.make_async_copy(states_hbm.at[0], states_vmem, load_sem.at[1]),
        pltpu.make_async_copy(lift_hbm, lift, load_sem.at[2]),
        pltpu.make_async_copy(gate_hbm, weights.at[s, 0], load_sem.at[3]),
        pltpu.make_async_copy(up_hbm, weights.at[s, 1], load_sem.at[4]),
        pltpu.make_async_copy(down_hbm, down.at[c], load_sem.at[5]),
        pltpu.make_async_copy(ret_hbm, ret, load_sem.at[6]),
    ]
    for load in loads:
        load.start()
    barrier = pltpu.get_barrier_semaphore()
    partners = [{"seq": slot(d)} for d in (1, -1, 2, -2)] + [{"seq": sib}]
    partners += [{"grp": xa}, {"grp": xb}, {"grp": (x + 2) % 4}]
    partners += [{"tp": z_at(d)} for d in range(1, 8)]
    for partner in partners:
        pl.semaphore_signal(barrier, inc=1, device_id=partner, device_id_type=MESH)

    pl.semaphore_wait(barrier, len(partners))

    def y_ref(q, way, hop):
        rows = pl.ds(0, 256) if hop < 3 else pl.ds(128 * way, 128)
        return weights.at[slot(q), :, rows]

    def y_go(way, hop):
        device = {"seq": slot(1 if way == 0 else -1)}
        if hop == 0:
            send(gate_hbm, weights.at[s, 0], y_sems, (way, 0), device)
            send(up_hbm, weights.at[s, 1], y_sems, (way, 4), device)
        else:
            ref = y_ref(-hop if way == 0 else hop, way, hop)
            send(ref, ref, y_sems, (way, hop), device)

    def sib_go(q):
        ref = weights.at[slot(q)]
        send(ref, ref, sib_sems, (q % 8,), {"seq": sib})

    def y_step(hop):
        for way in (0, 1):
            q = -(hop + 1) if way == 0 else hop + 1
            if hop == 0:
                arrived(weights.at[slot(q), 0], y_sems, (way, 0), {"seq": slot(1)})
                arrived(weights.at[slot(q), 1], y_sems, (way, 4), {"seq": slot(1)})
            else:
                arrived(y_ref(q, way, hop), y_sems, (way, hop), {"seq": slot(1)})
            if hop < 3:
                y_go(way, hop + 1)
                sib_go(q)
        if hop == 3:
            sib_go(4)

    def sib_wait():
        for k in range(8):
            arrived(weights.at[2 * ((y + k) % 8) + 1 - c], sib_sems, (k,), {"seq": sib})

    for k in (1, 2, 3):
        send(ret_hbm.at[y, :, x], ret_rows.at[k, :, x], rz_sems, (k,), {"tp": z_at(4 * c + k)})

    def across():
        return remote(ret_hbm.at[y, :, x], ret_rows.at[0, :, x], rz_sems, (0,), {"tp": z_at(4)})

    @pl.when(c == 1)
    def _():
        across().start()

    send(down_hbm, down.at[c], dn_sems, (0,), {"seq": sib})
    y_go(0, 0)
    y_go(1, 0)

    for load in loads[:2]:
        load.wait()
    onehot = (lax.broadcasted_iota(jnp.int32, (NMAX, 256), 0) == slots[...]).astype(F32)
    counts = jnp.sum(onehot, axis=1, keepdims=True)
    states = states_vmem[...]
    sums = dot(onehot.astype(BF16), states)
    pooled = (sums / jnp.maximum(counts, 1.0)).astype(BF16)
    loads[2].wait()

    def toward(way, d):
        return {"tp": z_at(d if way == 0 else -d)}

    def lift_go(way):
        sign = 1 if way == 0 else -1
        rows = pl.ds(32 * way, 32)
        send(lift_out.at[4, rows], lift_far.at[way], lift_sems, (way, 0), toward(way, 2))
        send(lift_out.at[3 * sign % 8], lift_in.at[way, 0], lift_sems, (way, 1), toward(way, 1))

    def lift_near(way):
        sign = 1 if way == 0 else -1
        send(lift_out.at[sign % 8], lift_in.at[way, 1], lift_sems, (way, 2), toward(way, 1))

    def lift_mid():
        for way in (0, 1):
            sign = 1 if way == 0 else -1
            arrived(lift_far.at[way], lift_sems, (way, 0), toward(way, 2))
            arrived(lift_in.at[way, 0], lift_sems, (way, 1), toward(way, 1))
            total = lift_out[2 * sign % 8].astype(F32) + lift_in[way, 0].astype(F32)
            far = lift_far[way].astype(F32)
            zero = jnp.zeros((32, 512), F32)
            far = jnp.concatenate([far, zero] if way == 0 else [zero, far], axis=0)
            lift_sum[way] = (total + far).astype(BF16)
            send(lift_sum.at[way], lift_in.at[way, 2], lift_sems, (way, 3), toward(way, 2))

    for d in (4, 3, 5, 1, 7, 2, 6, 0):
        columns = lift[:, pl.ds(pl.multiple_of(512 * z_at(d), 512), 512)]
        lift_out[d] = dot(pooled, columns).astype(BF16)
        if d == 5:
            lift_go(0)
            lift_go(1)
        if d == 7:
            lift_near(0)
            lift_near(1)
    onehot_t[...] = jnp.transpose(onehot).astype(BF16)
    for load in loads[3:]:
        load.wait()
    sib_go(0)

    @pl.when(c == 0)
    def _():
        ret_rows[0, :, x] = ret[y, :, x]

    def ret_x():
        for k in (1, 2, 3):
            arrived(ret_rows.at[k, :, x], rz_sems, (k,), {"tp": z_at(1)})

        @pl.when(c == 1)
        def _():
            across().wait_recv()

        for j in (2, 1, 3):
            ref = ret_rows.at[:, :, x]
            send(ref, ref, rx_sems, (j,), {"grp": (x + j) % 4})

    mine = pl.ds(4 * c, 4)

    def units(q):
        return pl.ds(32 * ((y + q + 8) % 8), 32)

    def far_units(way, q):
        return pl.ds(32 * ((y + q + 8) % 8) + 16 * way, 16)

    def along(way, d):
        return {"seq": slot(d if way == 0 else -d)}

    def dr_products():
        for j in (1, 3, 2):
            arrived(ret_rows.at[:, :, x], rx_sems, (j,), {"grp": xa})
        arrived(down.at[1 - c], dn_sems, (0,), {"seq": sib})
        for k in range(4):
            val = dot(down[0], ret_rows[k, 0].reshape(256, 128))
            val = val + dot(down[1], ret_rows[k, 1].reshape(256, 128))
            dr_half[k] = val.astype(BF16)
        for way in (0, 1):
            sign = 1 if way == 0 else -1
            send(dr_half.at[:, far_units(way, 4)], dr_far.at[way], dy_sems, (way, 0), along(way, 2))
            send(dr_half.at[:, units(3 * sign)], dr_in.at[way, 0], dy_sems, (way, 1), along(way, 1))
            send(dr_half.at[:, units(sign)], dr_in.at[way, 1], dy_sems, (way, 2), along(way, 1))

    def dr_mid():
        for way in (0, 1):
            sign = 1 if way == 0 else -1
            arrived(dr_far.at[way], dy_sems, (way, 0), along(way, 2))
            arrived(dr_in.at[way, 0], dy_sems, (way, 1), along(way, 1))
            total = dr_half[:, units(2 * sign)].astype(F32) + dr_in[way, 0].astype(F32)
            far = dr_far[way].astype(F32)
            zero = jnp.zeros((4, 16, 128), F32)
            far = jnp.concatenate([far, zero] if way == 0 else [zero, far], axis=1)
            dr_sum[way] = (total + far).astype(BF16)
            send(dr_sum.at[way], dr_in.at[way, 2], dy_sems, (way, 3), along(way, 2))

    def dr_total():
        total = dr_half[:, units(0)].astype(F32)
        for way in (0, 1):
            arrived(dr_in.at[way, 1], dy_sems, (way, 2), along(way, 1))
            arrived(dr_in.at[way, 2], dy_sems, (way, 3), along(way, 2))
            total = total + dr_in[way, 1].astype(F32) + dr_in[way, 2].astype(F32)
        dr[mine, units(0)] = total.astype(BF16)
        for way in (0, 1):
            ref = dr.at[mine, units(0)]
            for d in (2, 1):
                send(ref, ref, dg_sems, (way, d - 1), along(way, d))

    def dr_pass():
        for way in (0, 1):
            ref = dr.at[mine, units(-2 if way == 0 else 2)]
            arrived(ref, dg_sems, (way, 1), along(way, 2))
            half = dr.at[mine, far_units(way, -2 if way == 0 else 2)]
            send(half, half, dg_sems, (way, 3), along(way, 2))
            send(ref, ref, dg_sems, (way, 2), along(way, 1))

    def dr_share():
        for way in (0, 1):
            sign = 1 if way == 0 else -1
            arrived(dr.at[mine, units(-sign)], dg_sems, (way, 0), along(way, 1))
            arrived(dr.at[mine, units(-3 * sign)], dg_sems, (way, 2), along(way, 1))
            arrived(dr.at[mine, far_units(way, 4)], dg_sems, (way, 3), along(way, 2))
        send(dr.at[mine], dr.at[mine], dh_sems, (0,), {"seq": sib})

    def first_second(i):
        return ((xa, 1), (xb, 3)) if i % 2 == 0 else ((xb, 3), (xa, 1))

    def xg_one(i):
        e = IN_ORDER[i]
        (n1, j1), _ = first_second(i)
        send(patch.at[e, 0], patch.at[e, j1], xg_sems, (e, 0), {"grp": n1})

    def xg_two(i):
        e = IN_ORDER[i]
        (n1, j1), (n2, j2) = first_second(i)
        send(patch.at[e, 0], patch.at[e, j2], xg_sems, (e, 1), {"grp": n2})
        arrived(patch.at[e, j1], xg_sems, (e, 0), {"grp": n1})
        send(patch.at[e, j1], patch.at[e, 2], xg_sems, (e, 2), {"grp": n2})

    def xg_wait(i):
        e = IN_ORDER[i]
        _, (n2, j2) = first_second(i)
        arrived(patch.at[e, j2], xg_sems, (e, 1), {"grp": n2})
        arrived(patch.at[e, 2], xg_sems, (e, 2), {"grp": n2})

    def za_near():
        for way in (0, 1):
            e = 1 if way == 0 else 7
            arrived(patch.at[e, 0], za_sems, (way, 0), toward(way, 1))
            xg_one(1 + way)

    def za_mid():
        for way in (0, 1):
            e, e3 = ((2, 3), (6, 5))[way]
            rows = pl.ds(32 * way, 32)
            arrived(patch.at[e, 0], za_sems, (way, 1), toward(way, 2))
            send(patch.at[e, 0, rows], patch.at[4, 0, rows], za_sems, (way, 3), toward(way, 2))
            send(patch.at[e, 0], patch.at[e3, 0], za_sems, (way, 2), toward(way, 1))
            xg_one(3 + way)

    def za_far():
        for way in (0, 1):
            arrived(patch.at[3 if way == 0 else 5, 0], za_sems, (way, 2), toward(way, 1))
            xg_one(5 + way)
        for way in (0, 1):
            rows = pl.ds(32 * way, 32)
            arrived(patch.at[4, 0, rows], za_sems, (way, 3), toward(way, 2))
        xg_one(7)

    def patch_start():
        block = lift_out[0].astype(F32)
        for way in (0, 1):
            arrived(lift_in.at[way, 1], lift_sems, (way, 2), toward(way, 1))
            arrived(lift_in.at[way, 2], lift_sems, (way, 3), toward(way, 2))
            block = block + lift_in[way, 1].astype(F32) + lift_in[way, 2].astype(F32)
        patch[0, 0] = block.astype(BF16)
        for way in (0, 1):
            for d in (2, 1):
                e = d if way == 0 else 8 - d
                send(patch.at[0, 0], patch.at[e, 0], za_sems, (way, d - 1), toward(way, d))
        xg_one(0)

    ret_x()
    lift_mid()
    y_step(0)
    patch_start()
    dr_products()
    za_near()
    za_mid()
    xg_two(0)
    dr_mid()
    y_step(1)
    xg_two(1)
    xg_two(2)
    za_far()
    dr_total()
    xg_two(3)
    xg_two(4)
    y_step(2)
    dr_pass()
    xg_two(5)
    xg_two(6)
    xg_two(7)
    y_step(3)

    squares = jnp.zeros((256, 1), F32)
    returned = jnp.zeros((64, 128), F32)

    def multiply(i, squares, returned):
        xg_wait(i)
        e = IN_ORDER[i]
        kb = z_at(-e)
        rows = patch[e].reshape(256, 512)
        returned = returned + dot(patch[e, 0], ret[kb].reshape(512, 128))
        wide = rows.astype(F32)
        squares = squares + jnp.sum(wide * wide, axis=1, keepdims=True)
        for a in (0, 1):
            w = weights[pl.ds(2 * kb, 2), a].reshape(512, 256)
            if i == 0:
                acc[a] = dot(rows, w)
            else:
                acc[a] += dot(rows, w)
        return squares, returned

    sib_wait()
    for i in range(6):
        squares, returned = multiply(i, squares, returned)
    dr_share()
    for i in range(6, 8):
        squares, returned = multiply(i, squares, returned)

    scale = lax.rsqrt(squares * (1.0 / 4096) + EPS)
    gate = acc[0] * scale
    up = acc[1] * scale
    hidden = (gate / (1.0 + jnp.exp(-gate)) * up).astype(BF16)

    arrived(dr.at[pl.ds(4 - 4 * c, 4)], dh_sems, (0,), {"seq": sib})

    def down_one(i):
        for n in (0, 1):
            part[i, :, n] = dot(hidden, dr[2 * i + n]).astype(BF16).reshape(4, 64, 128)
        for j, n in ((2, (x + 2) % 4), (1, xa), (3, xb)):
            send(part.at[i, j], part_in.at[i, j], h_sems, (i, j), {"grp": n})

    def down_two(i):
        total = part[i, 0].astype(F32)
        for j in (1, 3, 2):
            arrived(part_in.at[i, j], h_sems, (i, j), {"grp": xa})
            total = total + part_in[i, j].astype(F32)
        for n in (0, 1):
            d = 2 * i + n
            if d == 0:
                own_total.append(total[n])
            else:
                back_out[d] = total[n].astype(BF16)
                send(back_out.at[d], back_in.at[d], b_sems, (d,), {"tp": z_at(-d)})

    own_total = []
    order = (2, 1, 3, 0)
    for i in order:
        down_one(i)
    for i in order:
        down_two(i)

    returned = returned + own_total[0]
    for d in (1, 7, 2, 6, 3, 5, 4):
        arrived(back_in.at[d], b_sems, (d,), {"tp": z_at(d)})
        returned = returned + back_in[d].astype(F32)
    returned = returned.astype(BF16)

    mixed = states_vmem[...].astype(F32) + dot(onehot_t[...], returned)
    square = mixed * mixed
    upper = square.astype(BF16)
    lower = (square - upper.astype(F32)).astype(BF16)
    ones = jnp.ones((8, 128), BF16)
    dims = (((1,), (1,)), ((), ()))
    sq_out[...] = lax.dot_general(ones, upper, dims, preferred_element_type=F32) + (
        lax.dot_general(ones, lower, dims, preferred_element_type=F32)
    )
    for d in (4, 3, 5, 2, 6, 1, 7):
        send(sq_out, sq_in.at[d], q_sems, (d,), {"tp": z_at(d)})
    total = sq_out[...]
    for d in (1, 7, 2, 6, 3, 5, 4):
        arrived(sq_in.at[d], q_sems, (d,), {"tp": z_at(d)})
        total = total + sq_in[d]
    inverse = lax.rsqrt(total[0:1] * (1.0 / DL) + EPS)
    inverse = jnp.transpose(jnp.broadcast_to(inverse, (128, 256)))
    out_ref[...] = (mixed * inverse).astype(BF16)

    @pl.when(c == 1)
    def _():
        across().wait_send()

    for copy in started:
        copy.wait_send()


def on_device(
    byte_states, patch_map, lift_weight, gate_weight, up_weight, down_weight, return_weight
):
    vmem = pl.BlockSpec(memory_space=pltpu.VMEM)
    hbm = pl.BlockSpec(memory_space=pl.ANY)
    dma = pltpu.SemaphoreType.DMA
    out = pl.pallas_call(
        kernel,
        out_shape=jax.ShapeDtypeStruct((256, 128), BF16),
        in_specs=[hbm] * 7,
        out_specs=vmem,
        scratch_shapes=[
            pltpu.VMEM((1, 256), jnp.int32),
            pltpu.VMEM((256, 128), BF16),
            pltpu.VMEM((256, 64), BF16),
            pltpu.VMEM((128, 4096), BF16),
            pltpu.VMEM((16, 2, 256, 256), BF16),
            pltpu.VMEM((8, 64, 512), BF16),
            pltpu.VMEM((2, 32, 512), BF16),
            pltpu.VMEM((2, 64, 512), BF16),
            pltpu.VMEM((2, 3, 64, 512), BF16),
            pltpu.VMEM((8, 4, 64, 512), BF16),
            pltpu.VMEM((2, 256, 256), F32),
            pltpu.VMEM((2, 256, 256), BF16),
            pltpu.VMEM((8, 2, 4, 64, 128), BF16),
            pltpu.VMEM((4, 2, 4, 64, 128), BF16),
            pltpu.VMEM((4, 256, 128), BF16),
            pltpu.VMEM((2, 4, 16, 128), BF16),
            pltpu.VMEM((2, 4, 32, 128), BF16),
            pltpu.VMEM((2, 3, 4, 32, 128), BF16),
            pltpu.VMEM((8, 256, 128), BF16),
            pltpu.VMEM((4, 4, 2, 64, 128), BF16),
            pltpu.VMEM((4, 4, 2, 64, 128), BF16),
            pltpu.VMEM((8, 64, 128), BF16),
            pltpu.VMEM((8, 64, 128), BF16),
            pltpu.VMEM((8, 256), F32),
            pltpu.VMEM((8, 8, 256), F32),
            dma((7,)),
            dma((2, 5)), dma((2, 5)),
            dma((8,)), dma((8,)),
            dma((2, 4)), dma((2, 4)),
            dma((2, 4)), dma((2, 4)),
            dma((8, 3)), dma((8, 3)),
            dma((4,)), dma((4,)),
            dma((4,)), dma((4,)),
            dma((1,)), dma((1,)),
            dma((2, 4)), dma((2, 4)),
            dma((2, 4)), dma((2, 4)),
            dma((1,)), dma((1,)),
            dma((4, 4)), dma((4, 4)),
            dma((8,)), dma((8,)),
            dma((8,)), dma((8,)),
        ],
        compiler_params=pltpu.CompilerParams(
            collective_id=0, has_side_effects=True, vmem_limit_bytes=64 * 1024 * 1024
        ),
    )(
        byte_states, patch_map, lift_weight, gate_weight, up_weight, down_weight,
        return_weight.reshape(8, 2, 4, 64, 128),
    )
    return out[None]


def solution(mesh):
    placed = (
        P("grp", "seq", "tp"),
        P("grp", "seq"),
        P("tp", None),
        P("seq", ("grp", "tp")),
        P("seq", ("grp", "tp")),
        P(("grp", "tp"), "seq"),
        P(None, "tp"),
    )
    return jax.shard_map(
        on_device, mesh=mesh, in_specs=placed, out_specs=P("grp", "seq", "tp"), check_vma=False
    )
```

```python
import jax
import jax.numpy as jnp
from jax import lax
from jax.experimental import pallas as pl
from jax.experimental.pallas import tpu as pltpu
from jax.sharding import PartitionSpec as P

DL = 1024
NMAX = 64
EPS = 1e-05
MESH = pl.DeviceIdType.MESH
F32 = jnp.float32
BF16 = jnp.bfloat16
IN_ORDER = (0, 1, 7, 2, 6, 3, 5, 4)


def dot(a, b):
    return jnp.dot(a, b, preferred_element_type=F32)


def kernel(
    states_hbm, map_hbm, lift_hbm, gate_hbm, up_hbm, down_hbm, ret_hbm, out_ref,
    slots, states_vmem, onehot_t, lift, weights, lift_out, lift_far, lift_sum, lift_in, patch, acc,
    down, ret, ret_rows, dr_half, dr_far, dr_sum, dr_in, dr, part, part_in, back_out, back_in, sq_out, sq_in,
    load_sem,
    y_sends, y_recvs,
    sib_sends, sib_recvs,
    lift_sends, lift_recvs,
    za_sends, za_recvs,
    xg_sends, xg_recvs,
    rz_sends, rz_recvs,
    rx_sends, rx_recvs,
    dn_sends, dn_recvs,
    dy_sends, dy_recvs,
    dg_sends, dg_recvs,
    dh_sends, dh_recvs,
    h_sends, h_recvs,
    b_sends, b_recvs,
    q_sends, q_recvs,
):
    x = lax.axis_index("grp")
    s = lax.axis_index("seq")
    z = lax.axis_index("tp")
    y = s // 2
    c = s % 2
    xa = x + 1 - 2 * (x % 2)
    xb = 3 - x
    sib = 2 * y + 1 - c
    started = []
    y_sems = (y_sends, y_recvs)
    sib_sems = (sib_sends, sib_recvs)
    lift_sems = (lift_sends, lift_recvs)
    za_sems = (za_sends, za_recvs)
    xg_sems = (xg_sends, xg_recvs)
    rz_sems = (rz_sends, rz_recvs)
    rx_sems = (rx_sends, rx_recvs)
    dn_sems = (dn_sends, dn_recvs)
    dy_sems = (dy_sends, dy_recvs)
    dg_sems = (dg_sends, dg_recvs)
    dh_sems = (dh_sends, dh_recvs)
    h_sems = (h_sends, h_recvs)
    b_sems = (b_sends, b_recvs)
    q_sems = (q_sends, q_recvs)

    def z_at(d):
        return (z + d + 8) % 8

    def slot(q):
        return 2 * ((y + q + 8) % 8) + c

    def remote(src, dst, sems, index, device):
        return pltpu.make_async_remote_copy(
            src_ref=src, dst_ref=dst, send_sem=sems[0].at[index], recv_sem=sems[1].at[index],
            device_id=device, device_id_type=MESH,
        )

    def send(src, dst, sems, index, device):
        copy = remote(src, dst, sems, index, device)
        copy.start()
        started.append(copy)

    def arrived(ref, sems, index, device):
        remote(ref, ref, sems, index, device).wait_recv()

    loads = [
        pltpu.make_async_copy(map_hbm, slots, load_sem.at[0]),
        pltpu.make_async_copy(states_hbm.at[0], states_vmem, load_sem.at[1]),
        pltpu.make_async_copy(lift_hbm, lift, load_sem.at[2]),
        pltpu.make_async_copy(gate_hbm, weights.at[s, 0], load_sem.at[3]),
        pltpu.make_async_copy(up_hbm, weights.at[s, 1], load_sem.at[4]),
        pltpu.make_async_copy(down_hbm, down.at[c], load_sem.at[5]),
        pltpu.make_async_copy(ret_hbm, ret, load_sem.at[6]),
    ]
    for load in loads:
        load.start()
    barrier = pltpu.get_barrier_semaphore()
    partners = [{"seq": slot(d)} for d in (1, -1, 2, -2)] + [{"seq": sib}]
    partners += [{"grp": xa}, {"grp": xb}, {"grp": (x + 2) % 4}]
    partners += [{"tp": z_at(d)} for d in range(1, 8)]
    for partner in partners:
        pl.semaphore_signal(barrier, inc=1, device_id=partner, device_id_type=MESH)

    pl.semaphore_wait(barrier, len(partners))

    def y_ref(q, way, hop):
        rows = pl.ds(0, 256) if hop < 3 else pl.ds(128 * way, 128)
        return weights.at[slot(q), :, rows]

    def y_go(way, hop):
        device = {"seq": slot(1 if way == 0 else -1)}
        if hop == 0:
            send(gate_hbm, weights.at[s, 0], y_sems, (way, 0), device)
            send(up_hbm, weights.at[s, 1], y_sems, (way, 4), device)
        else:
            ref = y_ref(-hop if way == 0 else hop, way, hop)
            send(ref, ref, y_sems, (way, hop), device)

    def sib_go(q):
        ref = weights.at[slot(q)]
        send(ref, ref, sib_sems, (q % 8,), {"seq": sib})

    def y_step(hop):
        for way in (0, 1):
            q = -(hop + 1) if way == 0 else hop + 1
            if hop == 0:
                arrived(weights.at[slot(q), 0], y_sems, (way, 0), {"seq": slot(1)})
                arrived(weights.at[slot(q), 1], y_sems, (way, 4), {"seq": slot(1)})
            else:
                arrived(y_ref(q, way, hop), y_sems, (way, hop), {"seq": slot(1)})
            if hop < 3:
                y_go(way, hop + 1)
                sib_go(q)
        if hop == 3:
            sib_go(4)

    def sib_wait():
        for k in range(8):
            arrived(weights.at[2 * ((y + k) % 8) + 1 - c], sib_sems, (k,), {"seq": sib})

    for k in (1, 2, 3):
        send(ret_hbm.at[y, :, x], ret_rows.at[k, :, x], rz_sems, (k,), {"tp": z_at(4 * c + k)})

    def across():
        return remote(ret_hbm.at[y, :, x], ret_rows.at[0, :, x], rz_sems, (0,), {"tp": z_at(4)})

    @pl.when(c == 1)
    def _():
        across().start()

    send(down_hbm, down.at[c], dn_sems, (0,), {"seq": sib})
    y_go(0, 0)
    y_go(1, 0)

    for load in loads[:2]:
        load.wait()
    onehot = (lax.broadcasted_iota(jnp.int32, (NMAX, 256), 0) == slots[...]).astype(F32)
    counts = jnp.sum(onehot, axis=1, keepdims=True)
    states = states_vmem[...]
    sums = dot(onehot.astype(BF16), states)
    pooled = (sums / jnp.maximum(counts, 1.0)).astype(BF16)
    loads[2].wait()

    def toward(way, d):
        return {"tp": z_at(d if way == 0 else -d)}

    def lift_go(way):
        sign = 1 if way == 0 else -1
        rows = pl.ds(32 * way, 32)
        send(lift_out.at[4, rows], lift_far.at[way], lift_sems, (way, 0), toward(way, 2))
        send(lift_out.at[3 * sign % 8], lift_in.at[way, 0], lift_sems, (way, 1), toward(way, 1))

    def lift_near(way):
        sign = 1 if way == 0 else -1
        send(lift_out.at[sign % 8], lift_in.at[way, 1], lift_sems, (way, 2), toward(way, 1))

    def lift_mid():
        for way in (0, 1):
            sign = 1 if way == 0 else -1
            arrived(lift_far.at[way], lift_sems, (way, 0), toward(way, 2))
            arrived(lift_in.at[way, 0], lift_sems, (way, 1), toward(way, 1))
            total = lift_out[2 * sign % 8].astype(F32) + lift_in[way, 0].astype(F32)
            far = lift_far[way].astype(F32)
            zero = jnp.zeros((32, 512), F32)
            far = jnp.concatenate([far, zero] if way == 0 else [zero, far], axis=0)
            lift_sum[way] = (total + far).astype(BF16)
            send(lift_sum.at[way], lift_in.at[way, 2], lift_sems, (way, 3), toward(way, 2))

    for d in (4, 3, 5, 1, 7, 2, 6, 0):
        columns = lift[:, pl.ds(pl.multiple_of(512 * z_at(d), 512), 512)]
        lift_out[d] = dot(pooled, columns).astype(BF16)
        if d == 5:
            lift_go(0)
            lift_go(1)
        if d == 7:
            lift_near(0)
            lift_near(1)
    onehot_t[...] = jnp.transpose(onehot).astype(BF16)
    for load in loads[3:]:
        load.wait()
    sib_go(0)

    @pl.when(c == 0)
    def _():
        ret_rows[0, :, x] = ret[y, :, x]

    def ret_x():
        for k in (1, 2, 3):
            arrived(ret_rows.at[k, :, x], rz_sems, (k,), {"tp": z_at(1)})

        @pl.when(c == 1)
        def _():
            across().wait_recv()

        for j in (2, 1, 3):
            ref = ret_rows.at[:, :, x]
            send(ref, ref, rx_sems, (j,), {"grp": (x + j) % 4})

    mine = pl.ds(4 * c, 4)

    def units(q):
        return pl.ds(32 * ((y + q + 8) % 8), 32)

    def far_units(way, q):
        return pl.ds(32 * ((y + q + 8) % 8) + 16 * way, 16)

    def along(way, d):
        return {"seq": slot(d if way == 0 else -d)}

    def dr_products():
        for j in (1, 3, 2):
            arrived(ret_rows.at[:, :, x], rx_sems, (j,), {"grp": xa})
        arrived(down.at[1 - c], dn_sems, (0,), {"seq": sib})
        for k in range(4):
            val = dot(down[0], ret_rows[k, 0].reshape(256, 128))
            val = val + dot(down[1], ret_rows[k, 1].reshape(256, 128))
            dr_half[k] = val.astype(BF16)
        for way in (0, 1):
            sign = 1 if way == 0 else -1
            send(dr_half.at[:, far_units(way, 4)], dr_far.at[way], dy_sems, (way, 0), along(way, 2))
            send(dr_half.at[:, units(3 * sign)], dr_in.at[way, 0], dy_sems, (way, 1), along(way, 1))
            send(dr_half.at[:, units(sign)], dr_in.at[way, 1], dy_sems, (way, 2), along(way, 1))

    def dr_mid():
        for way in (0, 1):
            sign = 1 if way == 0 else -1
            arrived(dr_far.at[way], dy_sems, (way, 0), along(way, 2))
            arrived(dr_in.at[way, 0], dy_sems, (way, 1), along(way, 1))
            total = dr_half[:, units(2 * sign)].astype(F32) + dr_in[way, 0].astype(F32)
            far = dr_far[way].astype(F32)
            zero = jnp.zeros((4, 16, 128), F32)
            far = jnp.concatenate([far, zero] if way == 0 else [zero, far], axis=1)
            dr_sum[way] = (total + far).astype(BF16)
            send(dr_sum.at[way], dr_in.at[way, 2], dy_sems, (way, 3), along(way, 2))

    def dr_total():
        total = dr_half[:, units(0)].astype(F32)
        for way in (0, 1):
            arrived(dr_in.at[way, 1], dy_sems, (way, 2), along(way, 1))
            arrived(dr_in.at[way, 2], dy_sems, (way, 3), along(way, 2))
            total = total + dr_in[way, 1].astype(F32) + dr_in[way, 2].astype(F32)
        dr[mine, units(0)] = total.astype(BF16)
        for way in (0, 1):
            ref = dr.at[mine, units(0)]
            for d in (2, 1):
                send(ref, ref, dg_sems, (way, d - 1), along(way, d))

    def dr_pass():
        for way in (0, 1):
            ref = dr.at[mine, units(-2 if way == 0 else 2)]
            arrived(ref, dg_sems, (way, 1), along(way, 2))
            half = dr.at[mine, far_units(way, -2 if way == 0 else 2)]
            send(half, half, dg_sems, (way, 3), along(way, 2))
            send(ref, ref, dg_sems, (way, 2), along(way, 1))

    def dr_share():
        for way in (0, 1):
            sign = 1 if way == 0 else -1
            arrived(dr.at[mine, units(-sign)], dg_sems, (way, 0), along(way, 1))
            arrived(dr.at[mine, units(-3 * sign)], dg_sems, (way, 2), along(way, 1))
            arrived(dr.at[mine, far_units(way, 4)], dg_sems, (way, 3), along(way, 2))
        send(dr.at[mine], dr.at[mine], dh_sems, (0,), {"seq": sib})

    def first_second(i):
        return ((xa, 1), (xb, 3)) if i % 2 == 0 else ((xb, 3), (xa, 1))

    def xg_one(i):
        e = IN_ORDER[i]
        (n1, j1), _ = first_second(i)
        send(patch.at[e, 0], patch.at[e, j1], xg_sems, (e, 0), {"grp": n1})

    def xg_two(i):
        e = IN_ORDER[i]
        (n1, j1), (n2, j2) = first_second(i)
        send(patch.at[e, 0], patch.at[e, j2], xg_sems, (e, 1), {"grp": n2})
        arrived(patch.at[e, j1], xg_sems, (e, 0), {"grp": n1})
        send(patch.at[e, j1], patch.at[e, 2], xg_sems, (e, 2), {"grp": n2})

    def xg_wait(i):
        e = IN_ORDER[i]
        _, (n2, j2) = first_second(i)
        arrived(patch.at[e, j2], xg_sems, (e, 1), {"grp": n2})
        arrived(patch.at[e, 2], xg_sems, (e, 2), {"grp": n2})

    def za_near():
        for way in (0, 1):
            e = 1 if way == 0 else 7
            arrived(patch.at[e, 0], za_sems, (way, 0), toward(way, 1))
            xg_one(1 + way)

    def za_mid():
        for way in (0, 1):
            e, e3 = ((2, 3), (6, 5))[way]
            rows = pl.ds(32 * way, 32)
            arrived(patch.at[e, 0], za_sems, (way, 1), toward(way, 2))
            send(patch.at[e, 0, rows], patch.at[4, 0, rows], za_sems, (way, 3), toward(way, 2))
            send(patch.at[e, 0], patch.at[e3, 0], za_sems, (way, 2), toward(way, 1))
            xg_one(3 + way)

    def za_far():
        for way in (0, 1):
            arrived(patch.at[3 if way == 0 else 5, 0], za_sems, (way, 2), toward(way, 1))
            xg_one(5 + way)
        for way in (0, 1):
            rows = pl.ds(32 * way, 32)
            arrived(patch.at[4, 0, rows], za_sems, (way, 3), toward(way, 2))
        xg_one(7)

    def patch_start():
        block = lift_out[0].astype(F32)
        for way in (0, 1):
            arrived(lift_in.at[way, 1], lift_sems, (way, 2), toward(way, 1))
            arrived(lift_in.at[way, 2], lift_sems, (way, 3), toward(way, 2))
            block = block + lift_in[way, 1].astype(F32) + lift_in[way, 2].astype(F32)
        patch[0, 0] = block.astype(BF16)
        for way in (0, 1):
            for d in (2, 1):
                e = d if way == 0 else 8 - d
                send(patch.at[0, 0], patch.at[e, 0], za_sems, (way, d - 1), toward(way, d))
        xg_one(0)

    ret_x()
    lift_mid()
    y_step(0)
    patch_start()
    dr_products()
    za_near()
    za_mid()
    xg_two(0)
    dr_mid()
    y_step(1)
    xg_two(1)
    xg_two(2)
    za_far()
    dr_total()
    xg_two(3)
    xg_two(4)
    y_step(2)
    dr_pass()
    xg_two(5)
    xg_two(6)
    xg_two(7)
    y_step(3)

    squares = jnp.zeros((256, 1), F32)

    def multiply(i, squares):
        xg_wait(i)
        e = IN_ORDER[i]
        kb = z_at(-e)
        rows = patch[e].reshape(256, 512)
        wide = rows.astype(F32)
        squares = squares + jnp.sum(wide * wide, axis=1, keepdims=True)
        for a in (0, 1):
            w = weights[pl.ds(2 * kb, 2), a].reshape(512, 256)
            if i == 0:
                acc[a] = dot(rows, w)
            else:
                acc[a] += dot(rows, w)
        return squares

    sib_wait()
    for i in range(6):
        squares = multiply(i, squares)
    dr_share()
    for i in range(6, 8):
        squares = multiply(i, squares)

    scale = lax.rsqrt(squares * (1.0 / 4096) + EPS)
    gate = acc[0] * scale
    up = acc[1] * scale
    hidden = (gate / (1.0 + jnp.exp(-gate)) * up).astype(BF16)

    arrived(dr.at[pl.ds(4 - 4 * c, 4)], dh_sems, (0,), {"seq": sib})

    def down_one(i):
        for n in (0, 1):
            part[i, :, n] = dot(hidden, dr[2 * i + n]).astype(BF16).reshape(4, 64, 128)
        for j, n in ((2, (x + 2) % 4), (1, xa), (3, xb)):
            send(part.at[i, j], part_in.at[i, j], h_sems, (i, j), {"grp": n})

    def down_two(i):
        total = part[i, 0].astype(F32)
        for j in (1, 3, 2):
            arrived(part_in.at[i, j], h_sems, (i, j), {"grp": xa})
            total = total + part_in[i, j].astype(F32)
        for n in (0, 1):
            d = 2 * i + n
            if d == 0:
                own_total.append(total[n])
            else:
                back_out[d] = total[n].astype(BF16)
                send(back_out.at[d], back_in.at[d], b_sems, (d,), {"tp": z_at(-d)})

    own_total = []
    order = (2, 1, 3, 0)
    for i in order:
        down_one(i)
    returned = jnp.zeros((64, 128), F32)
    for e in range(8):
        returned = returned + dot(patch[e, 0], ret[z_at(-e)].reshape(512, 128))
    for i in order:
        down_two(i)

    returned = returned + own_total[0]
    for d in (1, 7, 2, 6, 3, 5, 4):
        arrived(back_in.at[d], b_sems, (d,), {"tp": z_at(d)})
        returned = returned + back_in[d].astype(F32)
    returned = returned.astype(BF16)

    mixed = states_vmem[...].astype(F32) + dot(onehot_t[...], returned)
    square = mixed * mixed
    upper = square.astype(BF16)
    lower = (square - upper.astype(F32)).astype(BF16)
    ones = jnp.ones((8, 128), BF16)
    dims = (((1,), (1,)), ((), ()))
    sq_out[...] = lax.dot_general(ones, upper, dims, preferred_element_type=F32) + (
        lax.dot_general(ones, lower, dims, preferred_element_type=F32)
    )
    for d in (4, 3, 5, 2, 6, 1, 7):
        send(sq_out, sq_in.at[d], q_sems, (d,), {"tp": z_at(d)})
    total = sq_out[...]
    for d in (1, 7, 2, 6, 3, 5, 4):
        arrived(sq_in.at[d], q_sems, (d,), {"tp": z_at(d)})
        total = total + sq_in[d]
    inverse = lax.rsqrt(total[0:1] * (1.0 / DL) + EPS)
    inverse = jnp.transpose(jnp.broadcast_to(inverse, (128, 256)))
    out_ref[...] = (mixed * inverse).astype(BF16)

    @pl.when(c == 1)
    def _():
        across().wait_send()

    for copy in started:
        copy.wait_send()


def on_device(
    byte_states, patch_map, lift_weight, gate_weight, up_weight, down_weight, return_weight
):
    vmem = pl.BlockSpec(memory_space=pltpu.VMEM)
    hbm = pl.BlockSpec(memory_space=pl.ANY)
    dma = pltpu.SemaphoreType.DMA
    out = pl.pallas_call(
        kernel,
        out_shape=jax.ShapeDtypeStruct((256, 128), BF16),
        in_specs=[hbm] * 7,
        out_specs=vmem,
        scratch_shapes=[
            pltpu.VMEM((1, 256), jnp.int32),
            pltpu.VMEM((256, 128), BF16),
            pltpu.VMEM((256, 64), BF16),
            pltpu.VMEM((128, 4096), BF16),
            pltpu.VMEM((16, 2, 256, 256), BF16),
            pltpu.VMEM((8, 64, 512), BF16),
            pltpu.VMEM((2, 32, 512), BF16),
            pltpu.VMEM((2, 64, 512), BF16),
            pltpu.VMEM((2, 3, 64, 512), BF16),
            pltpu.VMEM((8, 4, 64, 512), BF16),
            pltpu.VMEM((2, 256, 256), F32),
            pltpu.VMEM((2, 256, 256), BF16),
            pltpu.VMEM((8, 2, 4, 64, 128), BF16),
            pltpu.VMEM((4, 2, 4, 64, 128), BF16),
            pltpu.VMEM((4, 256, 128), BF16),
            pltpu.VMEM((2, 4, 16, 128), BF16),
            pltpu.VMEM((2, 4, 32, 128), BF16),
            pltpu.VMEM((2, 3, 4, 32, 128), BF16),
            pltpu.VMEM((8, 256, 128), BF16),
            pltpu.VMEM((4, 4, 2, 64, 128), BF16),
            pltpu.VMEM((4, 4, 2, 64, 128), BF16),
            pltpu.VMEM((8, 64, 128), BF16),
            pltpu.VMEM((8, 64, 128), BF16),
            pltpu.VMEM((8, 256), F32),
            pltpu.VMEM((8, 8, 256), F32),
            dma((7,)),
            dma((2, 5)), dma((2, 5)),
            dma((8,)), dma((8,)),
            dma((2, 4)), dma((2, 4)),
            dma((2, 4)), dma((2, 4)),
            dma((8, 3)), dma((8, 3)),
            dma((4,)), dma((4,)),
            dma((4,)), dma((4,)),
            dma((1,)), dma((1,)),
            dma((2, 4)), dma((2, 4)),
            dma((2, 4)), dma((2, 4)),
            dma((1,)), dma((1,)),
            dma((4, 4)), dma((4, 4)),
            dma((8,)), dma((8,)),
            dma((8,)), dma((8,)),
        ],
        compiler_params=pltpu.CompilerParams(
            collective_id=0, has_side_effects=True, vmem_limit_bytes=64 * 1024 * 1024
        ),
    )(
        byte_states, patch_map, lift_weight, gate_weight, up_weight, down_weight,
        return_weight.reshape(8, 2, 4, 64, 128),
    )
    return out[None]


def solution(mesh):
    placed = (
        P("grp", "seq", "tp"),
        P("grp", "seq"),
        P("tp", None),
        P("seq", ("grp", "tp")),
        P("seq", ("grp", "tp")),
        P(("grp", "tp"), "seq"),
        P(None, "tp"),
    )
    return jax.shard_map(
        on_device, mesh=mesh, in_specs=placed, out_specs=P("grp", "seq", "tp"), check_vma=False
    )
```
